128 devices in a mesh: dp: 16 (over z, x), table: 8 (over y, core).
Axes of the slice: x: 4, y: 4, z: 4, core: 2. Of those that a mesh axis runs over, the one named last changes fastest.
Arguments:
- hot_grad: float32 [16, 8, 1024, 512], P('dp', 'table'), may hold values from -8 to 8
- first_moment: float32 [1024, 512], P('dp'), may hold values from -24 to 24
- second_moment: float32 [1024, 512], P('dp'), may hold values from 0.01 to 0.5
- hot_master: float32 [1024, 512], P('dp'), may hold values from -3 to 3
- hot_ids: int32 [16, 8, 4096], P('dp', 'table'), may hold values from 0 to 1023
- hot_lengths: int32 [16, 8, 1024], P('dp', 'table'), may hold values from 1 to 16, 4096 in all within a row
- cold_table: bfloat16 [16384, 512], P('table'), may hold values from -6 to 6
- cold_index: int32 [16, 8, 8, 128], P('dp', 'table'), may hold values from 0 to 2047
- cold_count: int32 [16, 8, 8], P('dp', 'table'), may hold values from 32 to 128, as said below
- cold_sample: int32 [16, 8, 8, 128], P('dp', 'table'), may hold values from 0 to 1023
- w_in: bfloat16 [1024, 2048], replicated, may hold values from -0.1875 to 0.1875
- b_in: float32 [2048], replicated, may hold values from -3 to 3
- w_out: bfloat16 [2048, 2048], replicated, may hold values from -0.125 to 0.125
- b_out: float32 [2048], replicated, may hold values from -3 to 3
Outputs:
- activations: float32 [16, 8, 1024, 2048], P('dp', 'table')
- new_master: float32 [1024, 512], P(('dp', 'table'))
- new_first: float32 [1024, 512], P(('dp', 'table'))
- new_second: float32 [1024, 512], P(('dp', 'table'))
The draws below stay inside these ranges and needn't reach their ends.
Inputs may be any that keep to these rules, and one draw needn't show every extreme that they name: `hot_lengths`: each device's lengths sum to 4096. `cold_count`: for every owner and dp index some requester's block is full.
All inputs are finite; a program needn't handle non-finite values.
Results may differ from the reference program's by a relative error of at most 0.0036.
Values may be sent and summed in bfloat16 or wider, within the bound.
No kernel may reach another device: no remote copies, remote signals or barrier semaphores. Data moves between devices by JAX's collectives and lax.ppermute only.
A program may use at most 128 MiB of HBM per device.

```python
import math
import jax
import jax.numpy as jnp
import numpy as np
from jax import lax

E = 512
H = 2048
BATCH_DEV = 1024
COLD_DEV = 2048
MAXBAG = 16
BLK = 128
HOT = 1024
LOOK_DEV = 4096
N_DP = 16
N_TABLE = 8


def draw_cold_count(key, part):
    key = jax.random.fold_in(key, 7)
    shape = (N_DP, N_TABLE, N_TABLE)
    base = jax.random.randint(key, shape, BLK // 4, BLK + 1)
    dp_pos = lax.broadcasted_iota(jnp.int32, shape, 0)
    owner_pos = lax.broadcasted_iota(jnp.int32, shape, 1)
    asker_pos = lax.broadcasted_iota(jnp.int32, shape, 2)
    full = asker_pos == (owner_pos + dp_pos) % N_TABLE
    return jnp.where(full, BLK, base).astype(jnp.int32)


def set_ends(drawn, key, smallest, largest):
    shape = drawn.shape
    index_at = [jax.random.randint(jax.random.fold_in(key, axis), (), 0, shape[axis]) for axis in range(len(shape))]
    drawn = drawn.at[tuple(index_at)].set(smallest)
    longest = shape.index(max(shape))
    index_at[longest] = (index_at[longest] + 1) % shape[longest]
    return drawn.at[tuple(index_at)].set(largest)


def with_spikes(values, rng, source, target, parts, factor):
    def block_of(axis_at):
        return (jnp.arange(values.shape[axis_at]) // (values.shape[axis_at] // parts)).reshape((-1,) + (1,) * (values.ndim - 1 - axis_at))

    one_side = jax.random.permutation(rng, parts)[block_of(target)]
    other_side = (block_of(target) + parts // 2) % parts
    return jnp.where((block_of(source) == one_side) | (block_of(source) == other_side), factor * values, values)


def shard_levels(rng, extent, pieces, low, largest):
    def one(axis_at, shards_of):
        draws = jax.random.uniform(jax.random.fold_in(jax.random.fold_in(rng, 6), axis_at), (shards_of,), jnp.float32, low / len(pieces), largest / len(pieces))
        return jnp.repeat(jnp.exp(draws), extent[axis_at] // shards_of).reshape((-1,) + (1,) * (len(extent) - axis_at - 1))

    gain = one(*pieces[0])
    for cut in pieces[1:]:
        gain = gain * one(*cut)
    return gain


def cumulative_ranks(number_of, lean):
    weights = [(1 << 20) // math.isqrt(grade ** lean) + 1 for grade in range(1, number_of + 1)]
    deviation = 1 + sum(weights) // (1 << 30)
    return np.cumsum(np.array([max(1, weight // deviation) for weight in weights]))


def skewed_ids(rng, extent, number_of, lean):
    table = cumulative_ranks(number_of, lean)
    pick = jax.random.randint(jax.random.fold_in(rng, 1), extent, 0, int(table[number_of - 1]))
    grade = jnp.searchsorted(jnp.asarray(table, jnp.int32), pick, side="right")
    return jax.random.permutation(jax.random.fold_in(rng, 2), number_of)[grade].astype(jnp.int32)


def split_up(amount, total, bound, slope):
    weights = [(1 << 20) // math.isqrt(rank ** slope) + 1 for rank in range(2, amount + 1)]
    rest, counts = total - bound - (amount - 1), [1] * (amount - 1)
    while rest > 0:
        candidates = [i for i in range(amount - 1) if counts[i] < bound]
        mass, budget = sum([weights[i] for i in candidates]), rest
        for i in candidates:
            more = min(bound - counts[i], max(1, budget * weights[i] // mass), rest)
            counts[i] = counts[i] + more
            rest = rest - more
    return np.array([bound] + counts)


def ragged(own_key, count, total, reach, lean):
    if count == 2:
        one = jax.random.randint(own_key, (), max(1, total - reach), min(reach, total - 1) + 1)
        return jnp.stack([one, total - one])
    sizes = jnp.asarray(split_up(count, total, reach, lean), jnp.int32)
    twos = (count - 1) // 2
    source_of, receiver = sizes[1:1 + 2 * twos:2], sizes[2:2 + 2 * twos:2]
    slack = jnp.minimum(source_of - 1, reach - receiver)
    shifted = jax.random.randint(jax.random.fold_in(own_key, 1), (twos,), 0, 1 << 20) % (slack + 1)
    sizes = sizes.at[1:1 + 2 * twos:2].set(source_of - shifted).at[2:2 + 2 * twos:2].set(receiver + shifted)
    return sizes[jax.random.permutation(jax.random.fold_in(own_key, 2), count)]


def gaussian(rng, extent, scale, limit, pieces=(), kind=jnp.bfloat16):
    loudness = shard_levels(rng, extent, pieces, -0.22, 0.18) if pieces else 1.0
    values = jax.random.normal(rng, extent, jnp.float32) * scale * loudness
    return jnp.minimum(jnp.maximum(values, -limit), limit).astype(kind)


def heavy_noise(key, dims, spread, reach, pieces, heavy, held_as=jnp.bfloat16):
    values = spread * jax.random.normal(key, dims, jnp.float32)
    if pieces:
        values = values * shard_levels(key, dims, pieces, -0.22, 0.18)
    return jnp.clip(with_spikes(values, jax.random.fold_in(key, 3), *heavy), -reach, reach).astype(held_as)


def setup_inputs(seed: int = 0) -> dict:
    splits = jax.random.split(jax.random.key(seed), 15)
    hot_grad = heavy_noise(splits[0], (N_DP, N_TABLE, HOT, E), 1.0, 8.0, ((0, 16), (1, 8)), (0, 2, 16, 2.0), jnp.float32)
    first_moment = gaussian(splits[1], (HOT, E), 4.0, 24.0, ((0, 16),), jnp.float32)
    second_moment = jnp.clip(jnp.exp(math.log(0.5) - 3.912023 * jax.random.uniform(splits[2], (HOT, E), jnp.float32) ** shard_levels(splits[2], (HOT, E), ((0, 16),), -0.2, 0.2)), 0.01, 0.5)
    hot_master = gaussian(splits[3], (HOT, E), 0.5, 3.0, ((0, 16),), jnp.float32)
    hot_ids = set_ends(skewed_ids(splits[4], (N_DP, N_TABLE, LOOK_DEV), HOT, 1), jax.random.fold_in(splits[4], 3), 0, HOT - 1).astype(jnp.int32)
    hot_lengths = jax.vmap(lambda own: ragged(own, BATCH_DEV, LOOK_DEV, MAXBAG, 1))(jax.random.split(splits[5], N_DP * N_TABLE)).reshape((N_DP, N_TABLE, BATCH_DEV)).astype(jnp.int32)
    cold_table = gaussian(splits[6], (N_TABLE * COLD_DEV, E), 1.0, 6.0, ((0, 8),))
    cold_index = set_ends(jax.random.randint(splits[7], (N_DP, N_TABLE, N_TABLE, BLK), 0, COLD_DEV), jax.random.fold_in(splits[7], 1), 0, COLD_DEV - 1).astype(jnp.int32)
    cold_count = draw_cold_count(jax.random.fold_in(splits[14], 71), 0)
    cold_sample = set_ends(jax.random.randint(splits[9], (N_DP, N_TABLE, N_TABLE, BLK), 0, BATCH_DEV), jax.random.fold_in(splits[9], 1), 0, BATCH_DEV - 1).astype(jnp.int32)
    w_in = gaussian(splits[10], (2 * E, H), (2 * E) ** -0.5, 0.1875)
    b_in = gaussian(splits[11], (H,), 0.5, 3.0, (), jnp.float32)
    w_out = gaussian(splits[12], (H, H), H ** -0.5, 0.125)
    b_out = gaussian(splits[13], (H,), 0.5, 3.0, (), jnp.float32)
    return {"hot_grad": hot_grad, "first_moment": first_moment, "second_moment": second_moment, "hot_master": hot_master, "hot_ids": hot_ids, "hot_lengths": hot_lengths, "cold_table": cold_table, "cold_index": cold_index, "cold_count": cold_count, "cold_sample": cold_sample, "w_in": w_in, "b_in": b_in, "w_out": w_out, "b_out": b_out}


beta_first = 0.9
beta_second = 0.999
adam_count = 10
learning_rate = 0.05
weight_decay = 0.01
epsilon = 1e-08

def adamw(master, first, second, grad):
    first_new = beta_first * first + (1.0 - beta_first) * grad
    second_new = beta_second * second + (1.0 - beta_second) * grad * grad
    corrected = first_new / (1.0 - beta_first ** adam_count)
    scaled = second_new / (1.0 - beta_second ** adam_count)
    master_new = master - learning_rate * (corrected / (jnp.sqrt(scaled) + epsilon) + weight_decay * master)
    return (master_new, first_new, second_new)

def reference(hot_grad, first_moment, second_moment, hot_master, hot_ids, hot_lengths, cold_table, cold_index, cold_count, cold_sample, w_in, b_in, w_out, b_out):
    grad = lax.optimization_barrier(jnp.sum(hot_grad, axis=(0, 1)))
    new_master, new_first, new_second = adamw(hot_master, first_moment, second_moment, grad)
    fresh = new_master.astype(jnp.bfloat16)
    owners = cold_index.shape[1]
    blocks = cold_index.shape[3]
    width = cold_table.shape[1]
    stacked = cold_table.reshape(owners, -1, width)
    owner_pos = jnp.arange(owners, dtype=jnp.int32)[None, :, None, None]
    sent = stacked[owner_pos, cold_index]
    slot_pos = jnp.arange(blocks, dtype=jnp.int32)
    used = slot_pos[None, None, None, :] < cold_count[..., None]
    sent = jnp.where(used[..., None], sent, jnp.zeros((), jnp.bfloat16))
    received = jnp.transpose(sent, (0, 2, 1, 3, 4))
    received = received.reshape(-1, owners * blocks, width)
    batch = hot_lengths.shape[2]
    look = hot_ids.shape[2]
    flat_ids = hot_ids.reshape(-1, look)
    flat_lengths = hot_lengths.reshape(-1, batch)
    flat_sample = cold_sample.reshape(-1, owners * blocks)

    def one_device(inputs):
        ids, lengths, rows_in, samples = inputs
        ends = jnp.cumsum(lengths)
        positions = jnp.arange(look, dtype=jnp.int32)
        segment = lax.optimization_barrier(jnp.sum((positions[:, None] >= ends[None, :]).astype(jnp.int32), axis=1))
        looked = fresh[ids].astype(jnp.float32)
        hot_pool = jax.ops.segment_sum(looked, segment, num_segments=batch)
        cold_pool = jax.ops.segment_sum(rows_in.astype(jnp.float32), samples, num_segments=batch)
        features = jnp.concatenate([hot_pool, cold_pool], axis=1).astype(jnp.bfloat16)
        pre = jnp.dot(features, w_in, preferred_element_type=jnp.float32) + b_in
        hidden = jnp.maximum(pre, 0.0).astype(jnp.bfloat16)
        return jnp.dot(hidden, w_out, preferred_element_type=jnp.float32) + b_out
    outputs = lax.map(one_device, (flat_ids, flat_lengths, received, flat_sample))
    activations = outputs.reshape(hot_ids.shape[0], hot_ids.shape[1], batch, -1)
    return (activations, new_master, new_first, new_second)
```

```python
import functools

import jax
import jax.numpy as jnp
from jax import lax
from jax.experimental import pallas as pl
from jax.experimental.pallas import tpu as pltpu
from jax.sharding import PartitionSpec as P

beta_first = 0.9
beta_second = 0.999
adam_count = 10
learning_rate = 0.05
weight_decay = 0.01
epsilon = 1e-08

CHUNK = 256
BAGS = 128


def adamw(master, first, second, grad):
    first_new = beta_first * first + (1.0 - beta_first) * grad
    second_new = beta_second * second + (1.0 - beta_second) * grad * grad
    corrected = first_new / (1.0 - beta_first**adam_count)
    scaled = second_new / (1.0 - beta_second**adam_count)
    master_new = master - learning_rate * (
        corrected / (jnp.sqrt(scaled) + epsilon) + weight_decay * master
    )
    return (master_new, first_new, second_new)


def count_kernel(columns_ref, lengths_ref, out_ref, start_ref, end_ref, total_ref):
    chunks = columns_ref.shape[0]
    blocks = lengths_ref.shape[0]
    width = out_ref.shape[1]
    row = lax.broadcasted_iota(jnp.int32, (BAGS, BAGS), 0)
    col = lax.broadcasted_iota(jnp.int32, (BAGS, BAGS), 1)
    upto = (col <= row).astype(jnp.bfloat16)
    before = (col < row).astype(jnp.bfloat16)
    contract = (((1,), (1,)), ((), ()))
    offset = jnp.float32(0.0)
    firsts = []
    for k in range(blocks):
        lengths = lengths_ref[k].astype(jnp.float32)
        spread = jnp.broadcast_to(lengths, (BAGS, BAGS)).astype(jnp.bfloat16)
        end_ref[k] = offset + lax.dot_general(
            upto, spread, contract, preferred_element_type=jnp.float32
        )
        start_ref[k] = offset + lax.dot_general(
            before, spread, contract, preferred_element_type=jnp.float32
        )
        firsts.append(offset)
        offset = offset + jnp.sum(lengths)
    total_ref[...] = jnp.zeros_like(total_ref)
    firsts = [f.astype(jnp.int32) for f in firsts]

    def chunk_step(j, _):
        ids = columns_ref[j]
        rows = lax.broadcasted_iota(jnp.int32, (width, CHUNK), 0)
        hits = jnp.where(rows == ids, 1.0, 0.0).astype(jnp.bfloat16)
        low = j * CHUNK
        k_low = jnp.int32(-1)
        k_high = jnp.int32(0)
        for f in firsts:
            k_low = k_low + (f <= low).astype(jnp.int32)
            k_high = k_high + (f < low + CHUNK).astype(jnp.int32)
        where = (low + lax.broadcasted_iota(jnp.int32, (BAGS, BAGS), 1)).astype(jnp.float32)

        def block_step(k, _):
            start, end = start_ref[k], end_ref[k]
            parts = [
                jnp.where((start <= where + o) & (where + o < end), 1.0, 0.0)
                for o in range(0, CHUNK, BAGS)
            ]
            member = jnp.concatenate(parts, axis=1).astype(jnp.bfloat16)
            place = pl.ds(pl.multiple_of(k * BAGS, BAGS), BAGS)
            total_ref[place, :] += lax.dot_general(
                member, hits, contract, preferred_element_type=jnp.float32
            )
            return 0

        lax.fori_loop(k_low, k_high, block_step, 0)
        return 0

    lax.fori_loop(0, chunks, chunk_step, 0)
    out_ref[...] = total_ref[...].astype(out_ref.dtype)


def count_matrix(columns, lengths, width):
    look, batch = columns.shape[0], lengths.shape[0]
    chunks, blocks = look // CHUNK, batch // BAGS
    return pl.pallas_call(
        count_kernel,
        out_shape=jax.ShapeDtypeStruct((batch, width), jnp.bfloat16),
        in_specs=[pl.BlockSpec(memory_space=pltpu.VMEM)] * 2,
        out_specs=pl.BlockSpec(memory_space=pltpu.VMEM),
        scratch_shapes=[
            pltpu.VMEM((blocks, BAGS, BAGS), jnp.float32),
            pltpu.VMEM((blocks, BAGS, BAGS), jnp.float32),
            pltpu.VMEM((batch, width), jnp.float32),
        ],
        compiler_params=pltpu.CompilerParams(vmem_limit_bytes=24 << 20),
        cost_estimate=pl.CostEstimate(
            flops=24 * 2 * BAGS * CHUNK * width, bytes_accessed=2 * batch * width, transcendentals=0
        ),
    )(columns.reshape(chunks, 1, CHUNK), lengths.reshape(blocks, 1, BAGS))


def on_device(
    hot_grad,
    first_moment,
    second_moment,
    hot_master,
    hot_ids,
    hot_lengths,
    cold_table,
    cold_index,
    cold_count,
    cold_sample,
    w_in,
    b_in,
    w_out,
    b_out,
):
    width = cold_table.shape[1]
    batch = hot_lengths.shape[2]
    hot = hot_grad.shape[2]
    n_dp, n_table = lax.axis_size("dp"), lax.axis_size("table")
    lines = n_table // 2
    place = lax.axis_index("table")
    core, line = place % 2, place // 2
    swap = [(i, i ^ 1) for i in range(n_table)]
    own = hot // (n_dp * n_table)

    grad = hot_grad[0, 0].reshape(n_dp, lines, 2, own, width)
    send = lax.dynamic_index_in_dim(grad, 1 - core, 2, keepdims=False).astype(jnp.bfloat16)
    keep = lax.dynamic_index_in_dim(grad, core, 2, keepdims=False)
    other = lax.ppermute(send, "table", swap)
    chip = (keep + other.astype(jnp.float32)).astype(jnp.bfloat16)
    parts = lax.all_to_all(chip, "dp", split_axis=0, concat_axis=0, tiled=True)
    share = jnp.sum(parts.reshape(n_dp, lines * own, width).astype(jnp.float32), axis=0)
    for step in range(1, lines):
        share_in = lax.ppermute(
            share, "table", [(i, (i + 2 * step) % n_table) for i in range(n_table)]
        )
        total = share_in + (share if step == 1 else total)

    def rows_of(state):
        state = state.reshape(lines, 2, own, width)
        return lax.dynamic_index_in_dim(state, core, 1, keepdims=False)

    updated = adamw(
        rows_of(hot_master), rows_of(first_moment), rows_of(second_moment),
        total.reshape(lines, own, width),
    )
    new_master, new_first, new_second = (
        lax.dynamic_index_in_dim(u, line, 0, keepdims=False) for u in updated
    )
    fresh = updated[0].astype(jnp.bfloat16).reshape(lines * own, width)
    spread = jnp.broadcast_to(fresh[None], (n_dp,) + fresh.shape)
    fresh_own = lax.all_to_all(spread, "dp", split_axis=0, concat_axis=0, tiled=True)
    fresh_own = fresh_own.reshape(hot // 2, width)
    fresh_other = lax.ppermute(fresh_own, "table", swap)

    index_rows = cold_index[0, 0]
    counts = cold_count[0, 0]
    picked = jnp.take(cold_table, index_rows, axis=0)
    slot_pos = lax.broadcasted_iota(jnp.int32, index_rows.shape, 1)
    used = slot_pos < counts[:, None]
    picked = jnp.where(used[..., None], picked, jnp.zeros((), jnp.bfloat16))
    received = lax.all_to_all(picked, "table", split_axis=0, concat_axis=0, tiled=True)
    samples = cold_sample[0, 0].reshape(-1)
    bag = lax.broadcasted_iota(jnp.int32, (batch, samples.shape[0]), 0)
    member = (bag == samples[None, :]).astype(jnp.bfloat16)
    cold_pool = jnp.dot(
        member, received.reshape(-1, width), preferred_element_type=jnp.float32
    )
    cold_feat = cold_pool.astype(jnp.bfloat16)
    cold_pre = jnp.dot(cold_feat, w_in[width:], preferred_element_type=jnp.float32) + b_in

    ids = hot_ids[0, 0]
    half = ((ids // own) % 2) ^ core
    columns = (ids // (2 * own)) * own + ids % own + half * (hot // 2)
    counted = count_matrix(columns, hot_lengths[0, 0], hot)

    hot_pool = jnp.dot(
        counted[:, : hot // 2], fresh_own, preferred_element_type=jnp.float32
    ) + jnp.dot(counted[:, hot // 2 :], fresh_other, preferred_element_type=jnp.float32)
    hot_feat = hot_pool.astype(jnp.bfloat16)
    pre = jnp.dot(hot_feat, w_in[:width], preferred_element_type=jnp.float32) + cold_pre
    hidden = jnp.maximum(pre, 0.0).astype(jnp.bfloat16)
    result = jnp.dot(hidden, w_out, preferred_element_type=jnp.float32) + b_out
    return (result[None, None], new_master, new_first, new_second)


def solution(mesh):
    return jax.shard_map(
        on_device,
        mesh=mesh,
        in_specs=(
            P("dp", "table", None, None),
            P("dp", None),
            P("dp", None),
            P("dp", None),
            P("dp", "table", None),
            P("dp", "table", None),
            P("table", None),
            P("dp", "table", None, None),
            P("dp", "table", None),
            P("dp", "table", None, None),
            P(),
            P(),
            P(),
            P(),
        ),
        out_specs=(
            P("dp", "table", None, None),
            P(("dp", "table"), None),
            P(("dp", "table"), None),
            P(("dp", "table"), None),
        ),
        check_vma=False,
    )
```

```python
import functools

import jax
import jax.numpy as jnp
from jax import lax
from jax.experimental import pallas as pl
from jax.experimental.pallas import tpu as pltpu
from jax.sharding import PartitionSpec as P

beta_first = 0.9
beta_second = 0.999
adam_count = 10
learning_rate = 0.05
weight_decay = 0.01
epsilon = 1e-08

BF16 = jnp.bfloat16
F32 = jnp.float32
I32 = jnp.int32
I16 = jnp.int16
VMEM = pl.BlockSpec(memory_space=pltpu.VMEM)
HBM = pl.BlockSpec(memory_space=pltpu.HBM)
MIB = 1 << 20
CHUNK = 512
BAGS = 256
LANES = 128
TILE = 256
ROWS = 512
PIECE = 512
LAST = (((1,), (1,)), ((), ()))
FIRST = (((0,), (0,)), ((), ()))


def adamw(master, first, second, grad):
    first_new = beta_first * first + (1.0 - beta_first) * grad
    second_new = beta_second * second + (1.0 - beta_second) * grad * grad
    corrected = first_new / (1.0 - beta_first**adam_count)
    scaled = second_new / (1.0 - beta_second**adam_count)
    master_new = master - learning_rate * (
        corrected / (jnp.sqrt(scaled) + epsilon) + weight_decay * master
    )
    return (master_new, first_new, second_new)


def dot(a, b):
    return jnp.dot(a, b, preferred_element_type=F32)


def dot_on(a, b, dims):
    return lax.dot_general(a, b, dims, preferred_element_type=F32)


def params(mib):
    return pltpu.CompilerParams(vmem_limit_bytes=mib * MIB)


def cost(flops, moved):
    return pl.CostEstimate(flops=flops, bytes_accessed=moved, transcendentals=0)


def in_hbm(array):
    return pltpu.with_memory_space_constraint(array, pltpu.HBM)


def my_place():
    place = lax.axis_index("table")
    return lax.rem(place, 2), lax.div(place, 2)


def after(first, *others):
    return lax.optimization_barrier((first, *others))[1:]


def load_half(grad_ref, side, held_ref, sems):
    steps = sems.shape[0]
    part = grad_ref.shape[0] // steps
    copies = []
    for i in range(steps):
        here = pl.ds(i * part, part)
        copy = pltpu.make_async_copy(
            grad_ref.at[here, :, side], held_ref.at[here], sems.at[i]
        )
        copy.start()
        copies.append(copy)
    return copies


def half_kernel(grad_ref, out_ref, held_ref, sems):
    core, _ = my_place()
    copies = load_half(grad_ref, 1 - core, held_ref, sems)
    rows, part = out_ref.shape[0] // len(copies), held_ref.shape[0] // len(copies)
    for i, copy in enumerate(copies):
        copy.wait()
        mine = held_ref[i * part : (i + 1) * part].reshape(rows, out_ref.shape[1])
        out_ref[i * rows : (i + 1) * rows, :] = mine.astype(BF16)


def chip_kernel(grad_ref, other_ref, out_ref, held_ref, sems):
    core, _ = my_place()
    copies = load_half(grad_ref, core, held_ref, sems)
    rows, part = out_ref.shape[0] // len(copies), held_ref.shape[0] // len(copies)
    for i, copy in enumerate(copies):
        copy.wait()
        here = slice(i * rows, (i + 1) * rows)
        mine = held_ref[i * part : (i + 1) * part].reshape(rows, out_ref.shape[1])
        out_ref[here, :] = (mine + other_ref[here, :].astype(F32)).astype(BF16)


def half_rows(grad, other=None):
    n_dp, lines, _, own, width = grad.shape
    total = n_dp * lines * own
    return pl.pallas_call(
        half_kernel if other is None else chip_kernel,
        out_shape=jax.ShapeDtypeStruct((total, width), BF16),
        in_specs=[HBM] if other is None else [HBM, VMEM],
        out_specs=VMEM,
        scratch_shapes=[
            pltpu.VMEM((n_dp, lines, own, width), F32), pltpu.SemaphoreType.DMA((4,))
        ],
        compiler_params=params(16),
        cost_estimate=cost(0, total * width * 6),
    )(in_hbm(grad), *(() if other is None else (other,)))


def sum_kernel(parts_ref, out_ref):
    total = parts_ref[0].astype(F32)
    for i in range(1, parts_ref.shape[0]):
        total = total + parts_ref[i].astype(F32)
    out_ref[...] = total


def sum_parts(parts):
    return pl.pallas_call(
        sum_kernel,
        out_shape=jax.ShapeDtypeStruct(parts.shape[1:], F32),
        in_specs=[VMEM],
        out_specs=VMEM,
        compiler_params=params(16),
        cost_estimate=cost(parts.size, parts.size * 2),
    )(parts)


def update_kernel(
    share_ref, in1_ref, in2_ref, in3_ref, master_ref, first_ref, second_ref,
    spread_ref, new_master_ref, new_first_ref, new_second_ref,
):
    core, line = my_place()
    lines, _, own, width = master_ref.shape
    grad = (share_ref[...] + in1_ref[...]) + (in2_ref[...] + in3_ref[...])
    rows = lines * own
    master, first, second = adamw(
        master_ref[:, core].reshape(rows, width),
        first_ref[:, core].reshape(rows, width),
        second_ref[:, core].reshape(rows, width),
        grad,
    )
    fresh = master.astype(BF16)
    for i in range(spread_ref.shape[0]):
        spread_ref[i] = fresh
    for whole, out_ref in (
        (master, new_master_ref), (first, new_first_ref), (second, new_second_ref)
    ):
        picked = whole[:own]
        for i in range(1, lines):
            picked = jnp.where(line == i, whole[i * own : (i + 1) * own], picked)
        out_ref[...] = picked


def update(share, shares_in, master, first, second, n_dp, lines, own):
    width = master.shape[1]
    rows = [a.reshape(lines, 2, own, width) for a in (master, first, second)]
    mine = jax.ShapeDtypeStruct((own, width), F32)
    return pl.pallas_call(
        update_kernel,
        out_shape=(
            jax.ShapeDtypeStruct((n_dp, lines * own, width), BF16), mine, mine, mine,
        ),
        in_specs=[VMEM] * 7,
        out_specs=(VMEM,) * 4,
        compiler_params=params(16),
        cost_estimate=cost(20 * share.size, 60 * share.size),
    )(share, *shares_in, *rows)


def pick_kernel(
    other_side, index_hbm, count_hbm, table_hbm, out_ref, index_ref, count_ref, table_ref, sems
):
    copies = [
        pltpu.make_async_copy(source, target, sems.at[i])
        for i, (source, target) in enumerate(
            ((index_hbm, index_ref), (count_hbm, count_ref), (table_hbm, table_ref))
        )
    ]
    for copy in copies:
        copy.start()
    core, line = my_place()
    side = 1 - core if other_side else core
    askers, slots = index_ref.shape
    lines = askers // 2
    rows = lax.broadcasted_iota(I16, (table_ref.shape[0], slots), 0)
    slot = lax.broadcasted_iota(I32, (1, slots), 1)
    each = lax.broadcasted_iota(I32, (1, askers), 1)
    copies[0].wait()
    copies[1].wait()
    for s in range(lines):
        asker = lax.rem(line + s, lines) * 2 + side
        used = jnp.sum(jnp.where(each == asker, count_ref[...], 0), axis=1, keepdims=True)
        wanted = index_ref[pl.ds(asker, 1), :]
        wanted = jnp.where(slot < used, wanted, -1).astype(I16)
        hit = jnp.where(rows == wanted, BF16(1), BF16(0))
        if s == 0:
            copies[2].wait()
        found = dot_on(hit, table_ref[...], FIRST)
        out_ref[s * slots : (s + 1) * slots, :] = found.astype(BF16)


def pick(index, counts, table, other_side):
    width = table.shape[1]
    rows = index.size // 2
    return pl.pallas_call(
        functools.partial(pick_kernel, other_side),
        out_shape=jax.ShapeDtypeStruct((rows, width), BF16),
        in_specs=[HBM, HBM, HBM],
        out_specs=VMEM,
        scratch_shapes=[
            pltpu.VMEM(index.shape, I32),
            pltpu.VMEM(counts.shape, I32),
            pltpu.VMEM(table.shape, BF16),
            pltpu.SemaphoreType.DMA((3,)),
        ],
        compiler_params=params(24),
        cost_estimate=cost(index.size * table.size, table.size * 2),
    )(in_hbm(index), in_hbm(counts), in_hbm(table))


def merge_kernel(near_ref, far_ref, *out_refs):
    slots = near_ref.shape[0] // len(out_refs)
    for s, out_ref in enumerate(out_refs):
        out_ref[:slots, :] = near_ref[s * slots : (s + 1) * slots, :]
        out_ref[slots:, :] = far_ref[s * slots : (s + 1) * slots, :]


def merge(near, far, lines):
    out = jax.ShapeDtypeStruct((2 * near.shape[0] // lines, near.shape[1]), BF16)
    return pl.pallas_call(
        merge_kernel,
        out_shape=(out,) * lines,
        in_specs=[VMEM, VMEM],
        out_specs=(VMEM,) * lines,
        compiler_params=params(16),
        cost_estimate=cost(0, near.size * 8),
    )(near, far)


def cold_kernel(sample_ref, *refs):
    rows_in, (w_hbm, b_ref, pre_hbm, w_ref, held_ref, sem, out_sems) = refs[:-7], refs[-7:]
    core, line = my_place()
    lines = len(rows_in)
    batch, width = held_ref.shape[0], rows_in[0].shape[1]
    copy = pltpu.make_async_copy(w_hbm.at[pl.ds(width, width)], w_ref, sem)
    copy.start()
    samples = []
    for s in range(lines):
        owner = lax.rem(line + lines - s, lines) * 2
        samples.append(
            jnp.concatenate(
                [sample_ref[pl.ds(owner + side, 1), :] for side in (core, 1 - core)], axis=1
            )
        )
    bag = lax.broadcasted_iota(I16, (TILE, samples[0].shape[1]), 0)

    def leave(i):
        here = pl.ds(pl.multiple_of(i * TILE, TILE), TILE)
        return pltpu.make_async_copy(held_ref.at[here], pre_hbm.at[here], out_sems.at[i])

    def step(i, _):
        pool = None
        for sample, rows_ref in zip(samples, rows_in, strict=True):
            hit = bag == (sample - i * TILE).astype(I16)
            part = dot(jnp.where(hit, BF16(1), BF16(0)), rows_ref[...])
            pool = part if pool is None else pool + part

        @pl.when(i == 0)
        def _():
            copy.wait()

        here = pl.ds(pl.multiple_of(i * TILE, TILE), TILE)
        held_ref[here, :] = (dot(pool.astype(BF16), w_ref[...]) + b_ref[...]).astype(BF16)
        leave(i).start()
        return 0

    lax.fori_loop(0, batch // TILE, step, 0)
    for i in range(batch // TILE):
        leave(i).wait()


def cold_half(samples, rows_in, w_in, b_in, batch):
    hidden = w_in.shape[1]
    width = rows_in[0].shape[1]
    return pl.pallas_call(
        cold_kernel,
        out_shape=pltpu.HBM((batch, hidden), BF16),
        in_specs=[VMEM] * (len(rows_in) + 1) + [HBM, VMEM],
        out_specs=HBM,
        scratch_shapes=[
            pltpu.VMEM((width, hidden), BF16),
            pltpu.VMEM((batch, hidden), BF16),
            pltpu.SemaphoreType.DMA(()),
            pltpu.SemaphoreType.DMA((batch // TILE,)),
        ],
        compiler_params=params(24),
        cost_estimate=cost(2 * batch * width * (hidden + samples.size), batch * hidden * 2),
    )(samples, *rows_in, in_hbm(w_in), b_in.reshape(1, hidden))


def count_kernel(low_block, own, ids_ref, lengths_ref, out_ref, total_ref):
    core, _ = my_place()
    bags, width = out_ref.shape
    row = lax.broadcasted_iota(I32, (BAGS, BAGS), 0)
    col = lax.broadcasted_iota(I32, (BAGS, BAGS), 1)
    upto = (col <= row).astype(BF16)
    before = (col < row).astype(BF16)
    rows = lax.broadcasted_iota(I16, (width, CHUNK), 0)
    offset = F32(0.0)
    if low_block:
        offset = jnp.sum(lengths_ref[:, : low_block * BAGS].astype(F32))
    for k in range(bags // BAGS):
        at = (low_block + k) * BAGS
        lengths = lengths_ref[:, at : at + BAGS].astype(F32)
        spread = jnp.broadcast_to(lengths, (LANES, BAGS)).astype(BF16)
        end = offset + dot_on(upto, spread, LAST)
        start = offset + dot_on(before, spread, LAST)
        following = offset + jnp.sum(lengths)
        lowest, highest = offset.astype(I32), following.astype(I32)
        offset = following
        total_ref[...] = jnp.zeros_like(total_ref)

        def step(j, _, start=start, end=end):
            here = pl.multiple_of(j * CHUNK, CHUNK)
            ids = ids_ref[:, pl.ds(here, CHUNK)]
            far = lax.div(ids, own) % 2 != core
            places = lax.div(ids, 2 * own) * own + lax.rem(ids, own)
            places = jnp.where(far, places + width // 2, places).astype(I16)
            hits = jnp.where(rows == places, BF16(1), BF16(0))
            lane = (here + lax.broadcasted_iota(I32, (BAGS, LANES), 1)).astype(F32)
            member = jnp.concatenate(
                [
                    jnp.where((start <= lane + o) & (lane + o < end), 1.0, 0.0)
                    for o in range(0, CHUNK, LANES)
                ],
                axis=1,
            ).astype(BF16)
            total_ref[...] += dot_on(member, hits, LAST)
            return 0

        lax.fori_loop(lowest // CHUNK, (highest + CHUNK - 1) // CHUNK, step, 0)
        out_ref[k * BAGS : (k + 1) * BAGS, :] = total_ref[...].astype(BF16)


def count_matrix(ids, lengths, width, own, low_block, blocks):
    return pl.pallas_call(
        functools.partial(count_kernel, low_block, own),
        out_shape=pltpu.HBM((blocks * BAGS, width), BF16),
        grid=(1,),
        in_specs=[VMEM, VMEM],
        out_specs=pl.BlockSpec((blocks * BAGS, width), lambda i: (0, 0)),
        scratch_shapes=[pltpu.VMEM((BAGS, width), F32)],
        compiler_params=params(24),
        cost_estimate=cost(3 * blocks * 2 * BAGS * CHUNK * width, 2 * blocks * BAGS * width),
    )(ids, lengths)


def own_kernel(
    low_hbm, high_hbm, own_ref, w_in_hbm, pool_ref, count_ref, w_hot_ref, held_ref, sems
):
    half, width = own_ref.shape
    low, high = low_hbm.shape[0], high_hbm.shape[0]
    mine, rest = pl.ds(0, half), pl.ds(half, half)
    copies = [
        pltpu.make_async_copy(source, target, sems.at[i])
        for i, (source, target) in enumerate(
            (
                (low_hbm.at[:, mine], held_ref.at[pl.ds(0, low)]),
                (high_hbm.at[:, mine], held_ref.at[pl.ds(low, high)]),
                (low_hbm.at[:, rest], count_ref.at[pl.ds(0, low)]),
                (high_hbm.at[:, rest], count_ref.at[pl.ds(low, high)]),
                (w_in_hbm.at[pl.ds(0, width)], w_hot_ref),
            )
        )
    ]
    for copy in copies:
        copy.start()
    copies[0].wait()
    copies[1].wait()

    def step(i, _):
        here = pl.ds(pl.multiple_of(i * TILE, TILE), TILE)
        pool_ref[here, :] = dot(held_ref[here, :], own_ref[...])
        return 0

    lax.fori_loop(0, (low + high) // TILE, step, 0)
    for copy in copies[2:]:
        copy.wait()


def own_pool(low, high, fresh_own, w_in):
    half, width = fresh_own.shape
    batch, hidden = low.shape[0] + high.shape[0], w_in.shape[1]
    return pl.pallas_call(
        own_kernel,
        out_shape=(
            pltpu.VMEM((batch, width), F32),
            pltpu.VMEM((batch, half), BF16),
            pltpu.VMEM((width, hidden), BF16),
        ),
        in_specs=[HBM, HBM, VMEM, HBM],
        out_specs=(VMEM, VMEM, VMEM),
        scratch_shapes=[pltpu.VMEM((batch, half), BF16), pltpu.SemaphoreType.DMA((5,))],
        compiler_params=params(16),
        cost_estimate=cost(2 * batch * half * width, 3 * batch * width * 4),
    )(in_hbm(low), in_hbm(high), fresh_own, in_hbm(w_in))


def mlp_kernel(
    pool_ref, count_ref, other_ref, w_hot_ref, pre_hbm, w_out_hbm, b_ref, out_hbm,
    hidden_ref, w_out_ref, pre_ref, out_ref, pre_sems, w_sems, out_sems,
):
    tiles, rows, _ = pre_ref.shape
    pieces, _, wide = w_out_ref.shape

    def load_pre(i):
        here = pl.ds(pl.multiple_of(i * rows, rows), rows)
        return pltpu.make_async_copy(pre_hbm.at[here], pre_ref.at[i], pre_sems.at[i])

    def load_w(n):
        here = pl.ds(pl.multiple_of(n * wide, wide), wide)
        return pltpu.make_async_copy(w_out_hbm.at[:, here], w_out_ref.at[n], w_sems.at[n])

    def leave(n):
        here = pl.ds(pl.multiple_of(n * wide, wide), wide)
        slot = lax.rem(n, 2)
        return pltpu.make_async_copy(out_ref.at[slot], out_hbm.at[:, here], out_sems.at[slot])

    for i in range(tiles):
        load_pre(i).start()
    for n in range(pieces):
        load_w(n).start()

    def first_layer(i, _):
        here = pl.ds(pl.multiple_of(i * rows, rows), rows)
        pool = pool_ref[here, :] + dot(count_ref[here, :], other_ref[...])
        load_pre(i).wait()
        pre = dot(pool.astype(BF16), w_hot_ref[...]) + pre_ref[i].astype(F32)
        hidden_ref[here, :] = jnp.maximum(pre, 0.0).astype(BF16)
        return 0

    lax.fori_loop(0, tiles, first_layer, 0)

    def second_layer(n, _):
        load_w(n).wait()

        @pl.when(n >= 2)
        def _():
            leave(n - 2).wait()

        here = pl.ds(pl.multiple_of(n * wide, wide), wide)
        out_ref[lax.rem(n, 2)] = dot(hidden_ref[...], w_out_ref[n]) + b_ref[:, here]
        leave(n).start()
        return 0

    lax.fori_loop(0, pieces, second_layer, 0)
    leave(pieces - 2).wait()
    leave(pieces - 1).wait()


def mlp(pool, counts, fresh_other, w_hot, pre, w_out, b_out):
    batch, hidden = pre.shape
    wide = w_out.shape[1]
    half, width = fresh_other.shape
    tiles, pieces = batch // ROWS, wide // PIECE
    return pl.pallas_call(
        mlp_kernel,
        out_shape=jax.ShapeDtypeStruct((batch, wide), F32),
        in_specs=[VMEM] * 4 + [HBM, HBM, VMEM],
        out_specs=HBM,
        scratch_shapes=[
            pltpu.VMEM((batch, hidden), BF16),
            pltpu.VMEM((pieces, hidden, PIECE), BF16),
            pltpu.VMEM((tiles, ROWS, hidden), BF16),
            pltpu.VMEM((2, batch, PIECE), F32),
            pltpu.SemaphoreType.DMA((tiles,)),
            pltpu.SemaphoreType.DMA((pieces,)),
            pltpu.SemaphoreType.DMA((2,)),
        ],
        compiler_params=params(36),
        cost_estimate=cost(
            2 * batch * (half * width + width * hidden + hidden * wide), batch * wide * 4
        ),
    )(
        pool, counts, fresh_other, w_hot, in_hbm(pre), in_hbm(w_out), b_out.reshape(1, wide)
    )


def on_device(
    hot_grad,
    first_moment,
    second_moment,
    hot_master,
    hot_ids,
    hot_lengths,
    cold_table,
    cold_index,
    cold_count,
    cold_sample,
    w_in,
    b_in,
    w_out,
    b_out,
):
    width = cold_table.shape[1]
    batch = hot_lengths.shape[2]
    hot = hot_grad.shape[2]
    n_dp, n_table = lax.axis_size("dp"), lax.axis_size("table")
    lines = n_table // 2
    own = hot // (n_dp * n_table)
    swap = [(i, i ^ 1) for i in range(n_table)]

    def along(array, step):
        pairs = [(i, (i + 2 * step) % n_table) for i in range(n_table)]
        return lax.ppermute(array, "table", pairs)

    grad = hot_grad[0, 0].reshape(n_dp, lines, 2, own, width)
    send = half_rows(grad)
    other = lax.ppermute(send, "table", swap)
    index, counts = cold_index[0, 0], cold_count[0]
    (index_far,) = after(send, index)
    far = pick(index_far, counts, cold_table, True)
    other, far = lax.optimization_barrier((other, far))
    chip = half_rows(grad, other)

    parts = lax.all_to_all(
        chip.reshape(n_dp, lines * own, width), "dp", split_axis=0, concat_axis=0, tiled=True
    )
    far_in = lax.ppermute(far, "table", swap)
    (index_near,) = after(chip, index)
    near = pick(index_near, counts, cold_table, False)
    blocks = merge(near, far_in, lines)
    rows_in = [along(blocks[s], s) if s in (1, lines - 1) else blocks[s] for s in range(lines)]

    ids, lengths = hot_ids[0], hot_lengths[0]
    early = batch // BAGS * 3 // 4
    (ids_now,) = after(blocks[0], ids)
    count_low = count_matrix(ids_now, lengths, hot, own, 0, early)
    parts, *_ = lax.optimization_barrier((parts, count_low, rows_in[1], rows_in[-1]))
    share = sum_parts(parts)
    shares_in = [along(share, s) for s in range(1, lines)]
    spread, new_master, new_first, new_second = update(
        share, shares_in, hot_master, first_moment, second_moment, n_dp, lines, own
    )
    fresh_own = lax.all_to_all(spread, "dp", split_axis=0, concat_axis=0, tiled=True)
    samples, ids_late, *middle = after(spread, cold_sample[0, 0], ids, *rows_in[2:-1])
    for s, block in enumerate(middle):
        rows_in[2 + s] = along(block, 2 + s)
    count_high = count_matrix(ids_late, lengths, hot, own, early, batch // BAGS - early)
    pre = cold_half(samples, rows_in, w_in, b_in, batch)
    fresh_own, *_ = lax.optimization_barrier((fresh_own, pre, count_high))
    fresh_own = fresh_own.reshape(hot // 2, width)
    fresh_other = lax.ppermute(fresh_own, "table", swap)
    pool, counts_other, w_hot = own_pool(count_low, count_high, fresh_own, w_in)
    fresh_other, pool = lax.optimization_barrier((fresh_other, pool))
    result = mlp(pool, counts_other, fresh_other, w_hot, pre, w_out, b_out)
    return (result[None, None], new_master, new_first, new_second)


def solution(mesh):
    return jax.shard_map(
        on_device,
        mesh=mesh,
        in_specs=(
            P("dp", "table", None, None),
            P("dp", None),
            P("dp", None),
            P("dp", None),
            P("dp", "table", None),
            P("dp", "table", None),
            P("table", None),
            P("dp", "table", None, None),
            P("dp", "table", None),
            P("dp", "table", None, None),
            P(),
            P(),
            P(),
            P(),
        ),
        out_specs=(
            P("dp", "table", None, None),
            P(("dp", "table"), None),
            P(("dp", "table"), None),
            P(("dp", "table"), None),
        ),
        check_vma=False,
    )
```

```python
import functools

import jax
import jax.numpy as jnp
from jax import lax
from jax.experimental import pallas as pl
from jax.experimental.pallas import tpu as pltpu
from jax.sharding import PartitionSpec as P

beta_first = 0.9
beta_second = 0.999
adam_count = 10
learning_rate = 0.05
weight_decay = 0.01
epsilon = 1e-08

BF16 = jnp.bfloat16
F32 = jnp.float32
I32 = jnp.int32
I16 = jnp.int16
VMEM = pl.BlockSpec(memory_space=pltpu.VMEM)
HBM = pl.BlockSpec(memory_space=pltpu.HBM)
MIB = 1 << 20
CHUNK = 512
BAGS = 256
LANES = 128
TILE = 256
ROWS = 512
PIECE = 512
LAST = (((1,), (1,)), ((), ()))
FIRST = (((0,), (0,)), ((), ()))


def adamw(master, first, second, grad):
    first_new = beta_first * first + (1.0 - beta_first) * grad
    second_new = beta_second * second + (1.0 - beta_second) * grad * grad
    corrected = first_new / (1.0 - beta_first**adam_count)
    scaled = second_new / (1.0 - beta_second**adam_count)
    master_new = master - learning_rate * (
        corrected / (jnp.sqrt(scaled) + epsilon) + weight_decay * master
    )
    return (master_new, first_new, second_new)


def dot(a, b):
    return jnp.dot(a, b, preferred_element_type=F32)


def dot_on(a, b, dims):
    return lax.dot_general(a, b, dims, preferred_element_type=F32)


def params(mib):
    return pltpu.CompilerParams(vmem_limit_bytes=mib * MIB)


def cost(flops, moved):
    return pl.CostEstimate(flops=flops, bytes_accessed=moved, transcendentals=0)


def in_hbm(array):
    return pltpu.with_memory_space_constraint(array, pltpu.HBM)


def my_place():
    place = lax.axis_index("table")
    return lax.rem(place, 2), lax.div(place, 2)


def after(first, *others):
    return lax.optimization_barrier((first, *others))[1:]


def load_half(grad_ref, side, held_ref, sems):
    steps = sems.shape[0]
    part = grad_ref.shape[0] // steps
    copies = []
    for i in range(steps):
        here = pl.ds(i * part, part)
        copy = pltpu.make_async_copy(
            grad_ref.at[here, :, side], held_ref.at[here], sems.at[i]
        )
        copy.start()
        copies.append(copy)
    return copies


def half_kernel(grad_ref, out_ref, held_ref, sems):
    core, _ = my_place()
    copies = load_half(grad_ref, 1 - core, held_ref, sems)
    rows, part = out_ref.shape[0] // len(copies), held_ref.shape[0] // len(copies)
    for i, copy in enumerate(copies):
        copy.wait()
        mine = held_ref[i * part : (i + 1) * part].reshape(rows, out_ref.shape[1])
        out_ref[i * rows : (i + 1) * rows, :] = mine.astype(BF16)


def other_half(grad):
    n_dp, lines, _, own, width = grad.shape
    total = n_dp * lines * own
    return pl.pallas_call(
        half_kernel,
        out_shape=jax.ShapeDtypeStruct((total, width), BF16),
        in_specs=[HBM],
        out_specs=VMEM,
        scratch_shapes=[
            pltpu.VMEM((n_dp, lines, own, width), F32), pltpu.SemaphoreType.DMA((4,))
        ],
        compiler_params=params(16),
        cost_estimate=cost(0, total * width * 6),
    )(in_hbm(grad))


def chip_kernel(mine_ref, other_ref, out_hbm, out_ref, sems):
    steps = sems.shape[0]
    rows, part = other_ref.shape[0] // steps, mine_ref.shape[0] // steps
    copies = []
    for i in range(steps):
        here = slice(i * rows, (i + 1) * rows)
        mine = mine_ref[i * part : (i + 1) * part].reshape(rows, out_ref.shape[1])
        out_ref[here, :] = (mine + other_ref[here, :].astype(F32)).astype(BF16)
        block = pl.ds(i * rows, rows)
        copy = pltpu.make_async_copy(out_ref.at[block], out_hbm.at[block], sems.at[i])
        copy.start()
        copies.append(copy)
    for copy in copies:
        copy.wait()


def chip_rows(mine, other):
    return pl.pallas_call(
        chip_kernel,
        out_shape=pltpu.HBM(other.shape, BF16),
        in_specs=[VMEM, VMEM],
        out_specs=HBM,
        scratch_shapes=[pltpu.VMEM(other.shape, BF16), pltpu.SemaphoreType.DMA((4,))],
        compiler_params=params(16),
        cost_estimate=cost(0, other.size * 8),
    )(mine, other)


def sum_kernel(parts_ref, out_ref):
    total = parts_ref[0].astype(F32)
    for i in range(1, parts_ref.shape[0]):
        total = total + parts_ref[i].astype(F32)
    out_ref[...] = total


def sum_parts(parts):
    return pl.pallas_call(
        sum_kernel,
        out_shape=jax.ShapeDtypeStruct(parts.shape[1:], F32),
        in_specs=[VMEM],
        out_specs=VMEM,
        compiler_params=params(16),
        cost_estimate=cost(parts.size, parts.size * 2),
    )(parts)


def update_kernel(
    share_ref, in1_ref, in2_ref, in3_ref, master_ref, first_ref, second_ref,
    spread_ref, new_master_ref, new_first_ref, new_second_ref,
):
    core, line = my_place()
    lines, _, own, width = master_ref.shape
    grad = (share_ref[...] + in1_ref[...]) + (in2_ref[...] + in3_ref[...])
    rows = lines * own
    master, first, second = adamw(
        master_ref[:, core].reshape(rows, width),
        first_ref[:, core].reshape(rows, width),
        second_ref[:, core].reshape(rows, width),
        grad,
    )
    fresh = master.astype(BF16)
    for i in range(spread_ref.shape[0]):
        spread_ref[i] = fresh
    for whole, out_ref in (
        (master, new_master_ref), (first, new_first_ref), (second, new_second_ref)
    ):
        picked = whole[:own]
        for i in range(1, lines):
            picked = jnp.where(line == i, whole[i * own : (i + 1) * own], picked)
        out_ref[...] = picked


def update(share, shares_in, master, first, second, n_dp, lines, own):
    width = master.shape[1]
    rows = [a.reshape(lines, 2, own, width) for a in (master, first, second)]
    mine = jax.ShapeDtypeStruct((own, width), F32)
    return pl.pallas_call(
        update_kernel,
        out_shape=(
            jax.ShapeDtypeStruct((n_dp, lines * own, width), BF16), mine, mine, mine,
        ),
        in_specs=[VMEM] * 7,
        out_specs=(VMEM,) * 4,
        compiler_params=params(16),
        cost_estimate=cost(20 * share.size, 60 * share.size),
    )(share, *shares_in, *rows)


def pick_kernel(other_side, index_hbm, count_hbm, table_hbm, *refs):
    if other_side:
        grad_hbm, out_ref, mine_ref, *scratch, grad_sems = refs
    else:
        out_ref, *scratch = refs
    index_ref, count_ref, table_ref, total_ref, sems = scratch
    asked = [
        pltpu.make_async_copy(index_hbm, index_ref, sems.at[0]),
        pltpu.make_async_copy(count_hbm, count_ref, sems.at[1]),
    ]
    pieces = sems.shape[0] - 2
    part = table_ref.shape[0] // pieces
    copies = [
        pltpu.make_async_copy(
            table_hbm.at[pl.ds(i * part, part)], table_ref.at[pl.ds(i * part, part)], sems.at[2 + i]
        )
        for i in range(pieces)
    ]
    for copy in asked + copies:
        copy.start()
    core, line = my_place()
    grads = load_half(grad_hbm, core, mine_ref, grad_sems) if other_side else []
    side = 1 - core if other_side else core
    askers, slots = index_ref.shape
    lines = askers // 2
    slot = lax.broadcasted_iota(I32, (1, slots), 1)
    each = lax.broadcasted_iota(I32, (1, askers), 1)
    for copy in asked:
        copy.wait()
    wanted = []
    for s in range(lines):
        asker = lax.rem(line + s, lines) * 2 + side
        used = jnp.sum(jnp.where(each == asker, count_ref[...], 0), axis=1, keepdims=True)
        wanted.append(jnp.where(slot < used, index_ref[pl.ds(asker, 1), :], -1).astype(I16))
    wanted = jnp.concatenate(wanted, axis=1)
    rows = lax.broadcasted_iota(I16, (part, lines * slots), 0)
    for i, copy in enumerate(copies):
        hit = jnp.where(rows + I16(i * part) == wanted, BF16(1), BF16(0))
        copy.wait()
        found = dot_on(hit, table_ref[i * part : (i + 1) * part, :], FIRST)
        if i > 0:
            found = found + total_ref[...]
        if i < pieces - 1:
            total_ref[...] = found
        else:
            out_ref[...] = found.astype(BF16)
    for copy in grads:
        copy.wait()


def pick(index, counts, table, grad=None):
    width = table.shape[1]
    rows = index.size // 2
    out = [jax.ShapeDtypeStruct((rows, width), BF16)]
    scratch = [
        pltpu.VMEM(index.shape, I32),
        pltpu.VMEM(counts.shape, I32),
        pltpu.VMEM(table.shape, BF16),
        pltpu.VMEM((rows, width), F32),
        pltpu.SemaphoreType.DMA((6,)),
    ]
    operands = [index, counts, table]
    if grad is not None:
        n_dp, lines, _, own, _ = grad.shape
        out.append(jax.ShapeDtypeStruct((n_dp, lines, own, width), F32))
        scratch.append(pltpu.SemaphoreType.DMA((4,)))
        operands.append(grad)
    return pl.pallas_call(
        functools.partial(pick_kernel, grad is not None),
        out_shape=tuple(out),
        in_specs=[HBM] * len(operands),
        out_specs=(VMEM,) * len(out),
        scratch_shapes=scratch,
        compiler_params=params(24),
        cost_estimate=cost(index.size * table.size, table.size * 2),
    )(*(in_hbm(a) for a in operands))


def merge_kernel(near_ref, far_ref, *out_refs):
    slots = near_ref.shape[0] // len(out_refs)
    for s, out_ref in enumerate(out_refs):
        out_ref[:slots, :] = near_ref[s * slots : (s + 1) * slots, :]
        out_ref[slots:, :] = far_ref[s * slots : (s + 1) * slots, :]


def merge(near, far, lines):
    out = jax.ShapeDtypeStruct((2 * near.shape[0] // lines, near.shape[1]), BF16)
    return pl.pallas_call(
        merge_kernel,
        out_shape=(out,) * lines,
        in_specs=[VMEM, VMEM],
        out_specs=(VMEM,) * lines,
        compiler_params=params(16),
        cost_estimate=cost(0, near.size * 8),
    )(near, far)


def cold_kernel(sample_ref, *refs):
    rows_in, rest = refs[:-8], refs[-8:]
    w_hbm, b_ref, pre_hbm, w_ref, feature_ref, held_ref, sem, out_sems = rest
    core, line = my_place()
    lines = len(rows_in)
    batch, width = feature_ref.shape
    copy = pltpu.make_async_copy(w_hbm.at[pl.ds(width, width)], w_ref, sem)
    copy.start()
    samples = []
    for s in range(lines):
        owner = lax.rem(line + lines - s, lines) * 2
        samples.append(
            jnp.concatenate(
                [sample_ref[pl.ds(owner + side, 1), :] for side in (core, 1 - core)], axis=1
            )
        )
    bag = lax.broadcasted_iota(I16, (ROWS, samples[0].shape[1]), 0)

    def pool_step(i, _):
        pool = None
        for sample, rows_ref in zip(samples, rows_in, strict=True):
            hit = bag == (sample - i * ROWS).astype(I16)
            part = dot(jnp.where(hit, BF16(1), BF16(0)), rows_ref[...])
            pool = part if pool is None else pool + part
        feature_ref[pl.ds(pl.multiple_of(i * ROWS, ROWS), ROWS), :] = pool.astype(BF16)
        return 0

    lax.fori_loop(0, batch // ROWS, pool_step, 0)
    copy.wait()

    def leave(i):
        here = pl.ds(pl.multiple_of(i * TILE, TILE), TILE)
        return pltpu.make_async_copy(held_ref.at[here], pre_hbm.at[here], out_sems.at[i])

    def step(i, _):
        here = pl.ds(pl.multiple_of(i * TILE, TILE), TILE)
        held_ref[here, :] = (dot(feature_ref[here, :], w_ref[...]) + b_ref[...]).astype(BF16)
        leave(i).start()
        return 0

    lax.fori_loop(0, batch // TILE, step, 0)
    for i in range(batch // TILE):
        leave(i).wait()


def cold_half(samples, rows_in, w_in, b_in, batch):
    hidden = w_in.shape[1]
    width = rows_in[0].shape[1]
    return pl.pallas_call(
        cold_kernel,
        out_shape=pltpu.HBM((batch, hidden), BF16),
        in_specs=[VMEM] * (len(rows_in) + 1) + [HBM, VMEM],
        out_specs=HBM,
        scratch_shapes=[
            pltpu.VMEM((width, hidden), BF16),
            pltpu.VMEM((batch, width), BF16),
            pltpu.VMEM((batch, hidden), BF16),
            pltpu.SemaphoreType.DMA(()),
            pltpu.SemaphoreType.DMA((batch // TILE,)),
        ],
        compiler_params=params(24),
        cost_estimate=cost(2 * batch * width * (hidden + samples.size), batch * hidden * 2),
    )(samples, *rows_in, in_hbm(w_in), b_in.reshape(1, hidden))


def count_kernel(low_block, own, ids_ref, lengths_ref, out_hbm, total_ref, out_ref, sems):
    core, _ = my_place()
    bags, width = out_ref.shape
    row = lax.broadcasted_iota(I32, (BAGS, BAGS), 0)
    col = lax.broadcasted_iota(I32, (BAGS, BAGS), 1)
    upto = (col <= row).astype(BF16)
    before = (col < row).astype(BF16)
    rows = lax.broadcasted_iota(I16, (width, CHUNK), 0)
    offset = F32(0.0)
    if low_block:
        offset = jnp.sum(lengths_ref[:, : low_block * BAGS].astype(F32))

    def leave(k):
        here = pl.ds(k * BAGS, BAGS)
        return pltpu.make_async_copy(out_ref.at[here], out_hbm.at[here], sems.at[k])

    for k in range(bags // BAGS):
        at = (low_block + k) * BAGS
        lengths = lengths_ref[:, at : at + BAGS].astype(F32)
        spread = jnp.broadcast_to(lengths, (LANES, BAGS)).astype(BF16)
        end = (offset + dot_on(upto, spread, LAST)).astype(I32).astype(I16)
        start = (offset + dot_on(before, spread, LAST)).astype(I32).astype(I16)
        following = offset + jnp.sum(lengths)
        lowest, highest = offset.astype(I32), following.astype(I32)
        offset = following
        total_ref[...] = jnp.zeros_like(total_ref)

        def step(j, _, start=start, end=end):
            here = pl.multiple_of(j * CHUNK, CHUNK)
            ids = ids_ref[:, pl.ds(here, CHUNK)]
            far = lax.div(ids, own) % 2 != core
            places = lax.div(ids, 2 * own) * own + lax.rem(ids, own)
            places = jnp.where(far, places + width // 2, places).astype(I16)
            hits = jnp.where(rows == places, BF16(1), BF16(0))
            lane = (here + lax.broadcasted_iota(I32, (1, CHUNK), 1)).astype(I16)
            parts = []
            for o in range(0, CHUNK, LANES):
                at_lane = lane[:, o : o + LANES]
                inside = (start <= at_lane) & (at_lane < end)
                parts.append(jnp.where(inside, BF16(1), BF16(0)))
            total_ref[...] += dot_on(jnp.concatenate(parts, axis=1), hits, LAST)
            return 0

        lax.fori_loop(lowest // CHUNK, (highest + CHUNK - 1) // CHUNK, step, 0)
        out_ref[k * BAGS : (k + 1) * BAGS, :] = total_ref[...].astype(BF16)
        leave(k).start()
    for k in range(bags // BAGS):
        leave(k).wait()


def count_matrix(ids, lengths, width, own, low_block, blocks):
    return pl.pallas_call(
        functools.partial(count_kernel, low_block, own),
        out_shape=pltpu.HBM((blocks * BAGS, width), BF16),
        in_specs=[VMEM, VMEM],
        out_specs=HBM,
        scratch_shapes=[
            pltpu.VMEM((BAGS, width), F32),
            pltpu.VMEM((blocks * BAGS, width), BF16),
            pltpu.SemaphoreType.DMA((blocks,)),
        ],
        compiler_params=params(24),
        cost_estimate=cost(3 * blocks * 2 * BAGS * CHUNK * width, 2 * blocks * BAGS * width),
    )(ids, lengths)


def own_kernel(own_ref, pre_hbm, w_in_hbm, *refs):
    counts, rest = refs[:-6], refs[-6:]
    pool_ref, count_ref, pre_ref, w_hot_ref, held_ref, sems = rest
    half = own_ref.shape[0]
    needed, later, low = [], [], 0
    for part in counts:
        here = pl.ds(low, part.shape[0])
        needed.append((part.at[:, pl.ds(0, half)], held_ref.at[here]))
        later.append((part.at[:, pl.ds(half, half)], count_ref.at[here]))
        low += part.shape[0]
    later.append((w_in_hbm.at[pl.ds(0, w_hot_ref.shape[0])], w_hot_ref))
    later.append((pre_hbm.at[pl.ds(0, pre_ref.shape[0])], pre_ref))
    copies = [
        pltpu.make_async_copy(source, target, sems.at[i])
        for i, (source, target) in enumerate(needed + later)
    ]
    for copy in copies:
        copy.start()
    for copy in copies[: len(counts)]:
        copy.wait()

    def step(i, _):
        here = pl.ds(pl.multiple_of(i * TILE, TILE), TILE)
        pool_ref[here, :] = dot(held_ref[here, :], own_ref[...])
        return 0

    lax.fori_loop(0, low // TILE, step, 0)
    for copy in copies[len(counts) :]:
        copy.wait()


def own_pool(counts, fresh_own, pre, w_in):
    half, width = fresh_own.shape
    batch, hidden = pre.shape
    return pl.pallas_call(
        own_kernel,
        out_shape=(
            pltpu.VMEM((batch, width), F32),
            pltpu.VMEM((batch, half), BF16),
            pltpu.VMEM((TILE, hidden), BF16),
            pltpu.VMEM((width, hidden), BF16),
        ),
        in_specs=[VMEM] + [HBM] * (2 + len(counts)),
        out_specs=(VMEM, VMEM, VMEM, VMEM),
        scratch_shapes=[
            pltpu.VMEM((batch, half), BF16), pltpu.SemaphoreType.DMA((2 * len(counts) + 2,))
        ],
        compiler_params=params(16),
        cost_estimate=cost(2 * batch * half * width, 3 * batch * width * 4),
    )(fresh_own, in_hbm(pre), in_hbm(w_in), *(in_hbm(c) for c in counts))


def mlp_kernel(
    pool_ref, count_ref, other_ref, w_hot_ref, first_pre_ref, pre_hbm, w_out_hbm, b_ref, out_hbm,
    hidden_ref, w_out_ref, pre_ref, out_ref, pre_sems, w_sems, out_sems,
):
    tiles = hidden_ref.shape[0] // TILE
    pieces, _, columns = w_out_ref.shape

    def load_pre(i):
        here = pl.ds(pl.multiple_of(i * TILE, TILE), TILE)
        return pltpu.make_async_copy(pre_hbm.at[here], pre_ref.at[i], pre_sems.at[i])

    def load_w(n):
        here = pl.ds(pl.multiple_of(n * columns, columns), columns)
        return pltpu.make_async_copy(w_out_hbm.at[:, here], w_out_ref.at[n], w_sems.at[n])

    def leave(n):
        here = pl.ds(pl.multiple_of(n * columns, columns), columns)
        slot = lax.rem(n, 2)
        return pltpu.make_async_copy(out_ref.at[slot], out_hbm.at[:, here], out_sems.at[slot])

    for i in range(1, tiles):
        load_pre(i).start()
    load_w(0).start()
    pre_ref[0] = first_pre_ref[...]

    def first_layer(i, _):
        here = pl.ds(pl.multiple_of(i * TILE, TILE), TILE)
        pool = pool_ref[here, :] + dot(count_ref[here, :], other_ref[...])

        @pl.when(i > 0)
        def _():
            load_pre(i).wait()

            @pl.when(i < pieces)
            def _():
                load_w(i).start()

        pre = dot(pool.astype(BF16), w_hot_ref[...]) + pre_ref[i].astype(F32)
        hidden_ref[here, :] = jnp.maximum(pre, 0.0).astype(BF16)
        return 0

    lax.fori_loop(0, tiles, first_layer, 0)

    def second_layer(n, _):
        load_w(n).wait()

        @pl.when(n >= 2)
        def _():
            leave(n - 2).wait()

        here = pl.ds(pl.multiple_of(n * columns, columns), columns)
        out_ref[lax.rem(n, 2)] = dot(hidden_ref[...], w_out_ref[n]) + b_ref[:, here]
        leave(n).start()
        return 0

    lax.fori_loop(0, pieces, second_layer, 0)
    leave(pieces - 2).wait()
    leave(pieces - 1).wait()


def mlp(pool, counts, fresh_other, w_hot, first_pre, pre, w_out, b_out):
    batch, hidden = pre.shape
    wide = w_out.shape[1]
    half, width = fresh_other.shape
    pieces = wide // PIECE
    return pl.pallas_call(
        mlp_kernel,
        out_shape=jax.ShapeDtypeStruct((batch, wide), F32),
        in_specs=[VMEM] * 5 + [HBM, HBM, VMEM],
        out_specs=HBM,
        scratch_shapes=[
            pltpu.VMEM((batch, hidden), BF16),
            pltpu.VMEM((pieces, hidden, PIECE), BF16),
            pltpu.VMEM((batch // TILE, TILE, hidden), BF16),
            pltpu.VMEM((2, batch, PIECE), F32),
            pltpu.SemaphoreType.DMA((batch // TILE,)),
            pltpu.SemaphoreType.DMA((pieces,)),
            pltpu.SemaphoreType.DMA((2,)),
        ],
        compiler_params=params(36),
        cost_estimate=cost(
            2 * batch * (half * width + width * hidden + hidden * wide), batch * wide * 4
        ),
    )(
        pool, counts, fresh_other, w_hot, first_pre, in_hbm(pre), in_hbm(w_out),
        b_out.reshape(1, wide),
    )


def on_device(
    hot_grad,
    first_moment,
    second_moment,
    hot_master,
    hot_ids,
    hot_lengths,
    cold_table,
    cold_index,
    cold_count,
    cold_sample,
    w_in,
    b_in,
    w_out,
    b_out,
):
    width = cold_table.shape[1]
    batch = hot_lengths.shape[2]
    hot = hot_grad.shape[2]
    n_dp, n_table = lax.axis_size("dp"), lax.axis_size("table")
    lines = n_table // 2
    own = hot // (n_dp * n_table)
    swap = [(i, i ^ 1) for i in range(n_table)]

    def along(array, step):
        pairs = [(i, (i + 2 * step) % n_table) for i in range(n_table)]
        return lax.ppermute(array, "table", pairs)

    grad = hot_grad[0, 0].reshape(n_dp, lines, 2, own, width)
    send = other_half(grad)
    other = lax.ppermute(send, "table", swap)
    index, counts = cold_index[0, 0], cold_count[0]
    (index_far,) = after(send, index)
    far, mine = pick(index_far, counts, cold_table, grad)
    chip = chip_rows(mine, other)

    parts = lax.all_to_all(
        chip.reshape(n_dp, lines * own, width), "dp", split_axis=0, concat_axis=0, tiled=True
    )
    far_in = lax.ppermute(far, "table", swap)
    (index_near,) = after(chip, index)
    (near,) = pick(index_near, counts, cold_table)
    blocks = merge(near, far_in, lines)
    rows_in = [along(blocks[s], s) if s in (1, lines - 1) else blocks[s] for s in range(lines)]

    ids, lengths = hot_ids[0], hot_lengths[0]
    blocks_in_all = batch // BAGS
    early = blocks_in_all * 3 // 4
    (ids_now,) = after(blocks[0], ids)
    count_low = count_matrix(ids_now, lengths, hot, own, 0, early)
    parts, *_ = lax.optimization_barrier((parts, count_low, rows_in[1], rows_in[-1]))
    share = sum_parts(parts)
    shares_in = [along(share, s) for s in range(1, lines)]
    spread, new_master, new_first, new_second = update(
        share, shares_in, hot_master, first_moment, second_moment, n_dp, lines, own
    )
    fresh_own = lax.all_to_all(spread, "dp", split_axis=0, concat_axis=0, tiled=True)
    samples, ids_late, *further = after(spread, cold_sample[0, 0], ids, *rows_in[2:-1])
    rows_in[2:-1] = [along(block, 2 + s) for s, block in enumerate(further)]
    count_high = count_matrix(ids_late, lengths, hot, own, early, blocks_in_all - early)
    pre = cold_half(samples, rows_in, w_in, b_in, batch)
    fresh_own, *_ = lax.optimization_barrier((fresh_own, pre, count_high))
    fresh_own = fresh_own.reshape(hot // 2, width)
    fresh_other = lax.ppermute(fresh_own, "table", swap)
    pool, counts_other, first_pre, w_hot = own_pool(
        [count_low, count_high], fresh_own, pre, w_in
    )
    fresh_other, pool = lax.optimization_barrier((fresh_other, pool))
    result = mlp(pool, counts_other, fresh_other, w_hot, first_pre, pre, w_out, b_out)
    return (result[None, None], new_master, new_first, new_second)


def solution(mesh):
    return jax.shard_map(
        on_device,
        mesh=mesh,
        in_specs=(
            P("dp", "table", None, None),
            P("dp", None),
            P("dp", None),
            P("dp", None),
            P("dp", "table", None),
            P("dp", "table", None),
            P("table", None),
            P("dp", "table", None, None),
            P("dp", "table", None),
            P("dp", "table", None, None),
            P(),
            P(),
            P(),
            P(),
        ),
        out_specs=(
            P("dp", "table", None, None),
            P(("dp", "table"), None),
            P(("dp", "table"), None),
            P(("dp", "table"), None),
        ),
        check_vma=False,
    )
```

```python
import functools

import jax
import jax.numpy as jnp
from jax import lax
from jax.experimental import pallas as pl
from jax.experimental.pallas import tpu as pltpu
from jax.sharding import PartitionSpec as P

beta_first = 0.9
beta_second = 0.999
adam_count = 10
learning_rate = 0.05
weight_decay = 0.01
epsilon = 1e-08

BF16 = jnp.bfloat16
F32 = jnp.float32
I32 = jnp.int32
I16 = jnp.int16
VMEM = pl.BlockSpec(memory_space=pltpu.VMEM)
HBM = pl.BlockSpec(memory_space=pltpu.HBM)
MIB = 1 << 20
CHUNK = 512
BAGS = 256
LANES = 128
TILE = 256
ROWS = 512
PIECE = 512
LAST = (((1,), (1,)), ((), ()))
FIRST = (((0,), (0,)), ((), ()))


def adamw(master, first, second, grad):
    first_new = beta_first * first + (1.0 - beta_first) * grad
    second_new = beta_second * second + (1.0 - beta_second) * grad * grad
    corrected = first_new / (1.0 - beta_first**adam_count)
    scaled = second_new / (1.0 - beta_second**adam_count)
    master_new = master - learning_rate * (
        corrected / (jnp.sqrt(scaled) + epsilon) + weight_decay * master
    )
    return (master_new, first_new, second_new)


def dot(a, b):
    return jnp.dot(a, b, preferred_element_type=F32)


def dot_on(a, b, dims):
    return lax.dot_general(a, b, dims, preferred_element_type=F32)


def params(mib):
    return pltpu.CompilerParams(vmem_limit_bytes=mib * MIB)


def cost(flops, moved):
    return pl.CostEstimate(flops=flops, bytes_accessed=moved, transcendentals=0)


def in_hbm(array):
    return pltpu.with_memory_space_constraint(array, pltpu.HBM)


def my_place():
    place = lax.axis_index("table")
    return lax.rem(place, 2), lax.div(place, 2)


def after(first, *others):
    return lax.optimization_barrier((first, *others))[1:]


def load_half(grad_ref, side, held_ref, sems):
    steps = sems.shape[0]
    part = grad_ref.shape[0] // steps
    copies = []
    for i in range(steps):
        here = pl.ds(i * part, part)
        copy = pltpu.make_async_copy(
            grad_ref.at[here, :, side], held_ref.at[here], sems.at[i]
        )
        copy.start()
        copies.append(copy)
    return copies


def half_kernel(grad_ref, out_ref, held_ref, sems):
    core, _ = my_place()
    copies = load_half(grad_ref, 1 - core, held_ref, sems)
    rows, part = out_ref.shape[0] // len(copies), held_ref.shape[0] // len(copies)
    for i, copy in enumerate(copies):
        copy.wait()
        mine = held_ref[i * part : (i + 1) * part].reshape(rows, out_ref.shape[1])
        out_ref[i * rows : (i + 1) * rows, :] = mine.astype(BF16)


def other_half(grad):
    n_dp, lines, _, own, width = grad.shape
    total = n_dp * lines * own
    return pl.pallas_call(
        half_kernel,
        out_shape=jax.ShapeDtypeStruct((total, width), BF16),
        in_specs=[HBM],
        out_specs=VMEM,
        scratch_shapes=[
            pltpu.VMEM((n_dp, lines, own, width), F32), pltpu.SemaphoreType.DMA((4,))
        ],
        compiler_params=params(16),
        cost_estimate=cost(0, total * width * 6),
    )(in_hbm(grad))


def chip_kernel(mine_ref, other_ref, out_hbm, out_ref, sems):
    steps = sems.shape[0]
    rows, part = other_ref.shape[0] // steps, mine_ref.shape[0] // steps
    copies = []
    for i in range(steps):
        here = slice(i * rows, (i + 1) * rows)
        mine = mine_ref[i * part : (i + 1) * part].reshape(rows, out_ref.shape[1])
        out_ref[here, :] = (mine + other_ref[here, :].astype(F32)).astype(BF16)
        block = pl.ds(i * rows, rows)
        copy = pltpu.make_async_copy(out_ref.at[block], out_hbm.at[block], sems.at[i])
        copy.start()
        copies.append(copy)
    for copy in copies:
        copy.wait()


def chip_rows(mine, other):
    return pl.pallas_call(
        chip_kernel,
        out_shape=pltpu.HBM(other.shape, BF16),
        in_specs=[VMEM, VMEM],
        out_specs=HBM,
        scratch_shapes=[pltpu.VMEM(other.shape, BF16), pltpu.SemaphoreType.DMA((4,))],
        compiler_params=params(16),
        cost_estimate=cost(0, other.size * 8),
    )(mine, other)


def sum_kernel(parts_ref, out_ref):
    total = parts_ref[0].astype(F32)
    for i in range(1, parts_ref.shape[0]):
        total = total + parts_ref[i].astype(F32)
    out_ref[...] = total


def sum_parts(parts):
    return pl.pallas_call(
        sum_kernel,
        out_shape=jax.ShapeDtypeStruct(parts.shape[1:], F32),
        in_specs=[VMEM],
        out_specs=VMEM,
        compiler_params=params(16),
        cost_estimate=cost(parts.size, parts.size * 2),
    )(parts)


def update_kernel(
    share_ref, in1_ref, in2_ref, in3_ref, master_ref, first_ref, second_ref,
    spread_ref, new_master_ref, new_first_ref, new_second_ref,
):
    core, line = my_place()
    lines, _, own, width = master_ref.shape
    grad = (share_ref[...] + in1_ref[...]) + (in2_ref[...] + in3_ref[...])
    rows = lines * own
    master, first, second = adamw(
        master_ref[:, core].reshape(rows, width),
        first_ref[:, core].reshape(rows, width),
        second_ref[:, core].reshape(rows, width),
        grad,
    )
    fresh = master.astype(BF16)
    for i in range(spread_ref.shape[0]):
        spread_ref[i] = fresh
    for whole, out_ref in (
        (master, new_master_ref), (first, new_first_ref), (second, new_second_ref)
    ):
        picked = whole[:own]
        for i in range(1, lines):
            picked = jnp.where(line == i, whole[i * own : (i + 1) * own], picked)
        out_ref[...] = picked


def update(share, shares_in, master, first, second, n_dp, lines, own):
    width = master.shape[1]
    rows = [a.reshape(lines, 2, own, width) for a in (master, first, second)]
    mine = jax.ShapeDtypeStruct((own, width), F32)
    return pl.pallas_call(
        update_kernel,
        out_shape=(
            jax.ShapeDtypeStruct((n_dp, lines * own, width), BF16), mine, mine, mine,
        ),
        in_specs=[VMEM] * 7,
        out_specs=(VMEM,) * 4,
        compiler_params=params(16),
        cost_estimate=cost(20 * share.size, 60 * share.size),
    )(share, *shares_in, *rows)


def pick_kernel(other_side, index_hbm, count_hbm, table_hbm, *refs):
    if other_side:
        grad_hbm, out_ref, mine_ref, *scratch, grad_sems = refs
    else:
        out_ref, *scratch = refs
    index_ref, count_ref, table_ref, total_ref, sems = scratch
    asked = [
        pltpu.make_async_copy(index_hbm, index_ref, sems.at[0]),
        pltpu.make_async_copy(count_hbm, count_ref, sems.at[1]),
    ]
    pieces = sems.shape[0] - 2
    part = table_ref.shape[0] // pieces
    copies = [
        pltpu.make_async_copy(
            table_hbm.at[pl.ds(i * part, part)], table_ref.at[pl.ds(i * part, part)], sems.at[2 + i]
        )
        for i in range(pieces)
    ]
    for copy in asked + copies:
        copy.start()
    core, line = my_place()
    grads = load_half(grad_hbm, core, mine_ref, grad_sems) if other_side else []
    side = 1 - core if other_side else core
    askers, slots = index_ref.shape
    lines = askers // 2
    slot = lax.broadcasted_iota(I32, (1, slots), 1)
    each = lax.broadcasted_iota(I32, (1, askers), 1)
    for copy in asked:
        copy.wait()
    wanted = []
    for s in range(lines):
        asker = lax.rem(line + s, lines) * 2 + side
        used = jnp.sum(jnp.where(each == asker, count_ref[...], 0), axis=1, keepdims=True)
        wanted.append(jnp.where(slot < used, index_ref[pl.ds(asker, 1), :], -1).astype(I16))
    wanted = jnp.concatenate(wanted, axis=1)
    rows = lax.broadcasted_iota(I16, (part, lines * slots), 0)
    for i, copy in enumerate(copies):
        hit = jnp.where(rows + I16(i * part) == wanted, BF16(1), BF16(0))
        copy.wait()
        found = dot_on(hit, table_ref[i * part : (i + 1) * part, :], FIRST)
        if i > 0:
            found = found + total_ref[...]
        if i < pieces - 1:
            total_ref[...] = found
        else:
            out_ref[...] = found.astype(BF16)
    for copy in grads:
        copy.wait()


def pick(index, counts, table, grad=None):
    width = table.shape[1]
    rows = index.size // 2
    out = [jax.ShapeDtypeStruct((rows, width), BF16)]
    scratch = [
        pltpu.VMEM(index.shape, I32),
        pltpu.VMEM(counts.shape, I32),
        pltpu.VMEM(table.shape, BF16),
        pltpu.VMEM((rows, width), F32),
        pltpu.SemaphoreType.DMA((6,)),
    ]
    operands = [index, counts, table]
    if grad is not None:
        n_dp, lines, _, own, _ = grad.shape
        out.append(jax.ShapeDtypeStruct((n_dp, lines, own, width), F32))
        scratch.append(pltpu.SemaphoreType.DMA((4,)))
        operands.append(grad)
    return pl.pallas_call(
        functools.partial(pick_kernel, grad is not None),
        out_shape=tuple(out),
        in_specs=[HBM] * len(operands),
        out_specs=(VMEM,) * len(out),
        scratch_shapes=scratch,
        compiler_params=params(24),
        cost_estimate=cost(index.size * table.size, table.size * 2),
    )(*(in_hbm(a) for a in operands))


def merge_kernel(near_ref, far_ref, *out_refs):
    slots = near_ref.shape[0] // len(out_refs)
    for s, out_ref in enumerate(out_refs):
        out_ref[:slots, :] = near_ref[s * slots : (s + 1) * slots, :]
        out_ref[slots:, :] = far_ref[s * slots : (s + 1) * slots, :]


def merge(near, far, lines):
    out = jax.ShapeDtypeStruct((2 * near.shape[0] // lines, near.shape[1]), BF16)
    return pl.pallas_call(
        merge_kernel,
        out_shape=(out,) * lines,
        in_specs=[VMEM, VMEM],
        out_specs=(VMEM,) * lines,
        compiler_params=params(16),
        cost_estimate=cost(0, near.size * 8),
    )(near, far)


def cold_kernel(sample_ref, *refs):
    rows_in, rest = refs[:-8], refs[-8:]
    w_hbm, b_ref, pre_hbm, w_ref, feature_ref, held_ref, sem, out_sems = rest
    core, line = my_place()
    lines = len(rows_in)
    batch, width = feature_ref.shape
    copy = pltpu.make_async_copy(w_hbm.at[pl.ds(width, width)], w_ref, sem)
    copy.start()
    samples = []
    for s in range(lines):
        owner = lax.rem(line + lines - s, lines) * 2
        samples.append(
            jnp.concatenate(
                [sample_ref[pl.ds(owner + side, 1), :] for side in (core, 1 - core)], axis=1
            )
        )
    bag = lax.broadcasted_iota(I16, (ROWS, samples[0].shape[1]), 0)

    def pool_step(i, _):
        pool = None
        for sample, rows_ref in zip(samples, rows_in, strict=True):
            hit = bag == (sample - i * ROWS).astype(I16)
            part = dot(jnp.where(hit, BF16(1), BF16(0)), rows_ref[...])
            pool = part if pool is None else pool + part
        feature_ref[pl.ds(pl.multiple_of(i * ROWS, ROWS), ROWS), :] = pool.astype(BF16)
        return 0

    lax.fori_loop(0, batch // ROWS, pool_step, 0)
    copy.wait()

    def leave(i):
        here = pl.ds(pl.multiple_of(i * TILE, TILE), TILE)
        return pltpu.make_async_copy(held_ref.at[here], pre_hbm.at[here], out_sems.at[i])

    def step(i, _):
        here = pl.ds(pl.multiple_of(i * TILE, TILE), TILE)
        held_ref[here, :] = (dot(feature_ref[here, :], w_ref[...]) + b_ref[...]).astype(BF16)
        leave(i).start()
        return 0

    lax.fori_loop(0, batch // TILE, step, 0)
    for i in range(batch // TILE):
        leave(i).wait()


def cold_half(samples, rows_in, w_in, b_in, batch):
    hidden = w_in.shape[1]
    width = rows_in[0].shape[1]
    return pl.pallas_call(
        cold_kernel,
        out_shape=pltpu.HBM((batch, hidden), BF16),
        in_specs=[VMEM] * (len(rows_in) + 1) + [HBM, VMEM],
        out_specs=HBM,
        scratch_shapes=[
            pltpu.VMEM((width, hidden), BF16),
            pltpu.VMEM((batch, width), BF16),
            pltpu.VMEM((batch, hidden), BF16),
            pltpu.SemaphoreType.DMA(()),
            pltpu.SemaphoreType.DMA((batch // TILE,)),
        ],
        compiler_params=params(24),
        cost_estimate=cost(2 * batch * width * (hidden + samples.size), batch * hidden * 2),
    )(samples, *rows_in, in_hbm(w_in), b_in.reshape(1, hidden))


def count_kernel(low_block, own, ids_ref, lengths_ref, out_hbm, total_ref, out_ref, sems):
    core, _ = my_place()
    bags, width = out_ref.shape
    row = lax.broadcasted_iota(I32, (BAGS, BAGS), 0)
    col = lax.broadcasted_iota(I32, (BAGS, BAGS), 1)
    upto = (col <= row).astype(BF16)
    before = (col < row).astype(BF16)
    rows = lax.broadcasted_iota(I16, (width, CHUNK), 0)
    offset = F32(0.0)
    if low_block:
        offset = jnp.sum(lengths_ref[:, : low_block * BAGS].astype(F32))

    def leave(k):
        here = pl.ds(k * BAGS, BAGS)
        return pltpu.make_async_copy(out_ref.at[here], out_hbm.at[here], sems.at[k])

    for k in range(bags // BAGS):
        at = (low_block + k) * BAGS
        lengths = lengths_ref[:, at : at + BAGS].astype(F32)
        spread = jnp.broadcast_to(lengths, (LANES, BAGS)).astype(BF16)
        end = (offset + dot_on(upto, spread, LAST)).astype(I32).astype(I16)
        start = (offset + dot_on(before, spread, LAST)).astype(I32).astype(I16)
        following = offset + jnp.sum(lengths)
        lowest, highest = offset.astype(I32), following.astype(I32)
        offset = following
        total_ref[...] = jnp.zeros_like(total_ref)

        def step(j, _, start=start, end=end):
            here = pl.multiple_of(j * CHUNK, CHUNK)
            ids = ids_ref[:, pl.ds(here, CHUNK)]
            far = lax.div(ids, own) % 2 != core
            places = lax.div(ids, 2 * own) * own + lax.rem(ids, own)
            places = jnp.where(far, places + width // 2, places).astype(I16)
            hits = jnp.where(rows == places, BF16(1), BF16(0))
            lane = (here + lax.broadcasted_iota(I32, (1, CHUNK), 1)).astype(I16)
            parts = []
            for o in range(0, CHUNK, LANES):
                at_lane = lane[:, o : o + LANES]
                inside = (start <= at_lane) & (at_lane < end)
                parts.append(jnp.where(inside, BF16(1), BF16(0)))
            total_ref[...] += dot_on(jnp.concatenate(parts, axis=1), hits, LAST)
            return 0

        lax.fori_loop(lowest // CHUNK, (highest + CHUNK - 1) // CHUNK, step, 0)
        out_ref[k * BAGS : (k + 1) * BAGS, :] = total_ref[...].astype(BF16)
        leave(k).start()
    for k in range(bags // BAGS):
        leave(k).wait()


def count_matrix(ids, lengths, width, own, low_block, blocks):
    return pl.pallas_call(
        functools.partial(count_kernel, low_block, own),
        out_shape=pltpu.HBM((blocks * BAGS, width), BF16),
        in_specs=[VMEM, VMEM],
        out_specs=HBM,
        scratch_shapes=[
            pltpu.VMEM((BAGS, width), F32),
            pltpu.VMEM((blocks * BAGS, width), BF16),
            pltpu.SemaphoreType.DMA((blocks,)),
        ],
        compiler_params=params(24),
        cost_estimate=cost(3 * blocks * 2 * BAGS * CHUNK * width, 2 * blocks * BAGS * width),
    )(ids, lengths)


def own_kernel(own_ref, pre_hbm, w_in_hbm, *refs):
    counts, rest = refs[:-6], refs[-6:]
    pool_ref, count_ref, pre_ref, w_hot_ref, held_ref, sems = rest
    half = own_ref.shape[0]
    needed, later, low = [], [], 0
    for part in counts:
        here = pl.ds(low, part.shape[0])
        needed.append((part.at[:, pl.ds(0, half)], held_ref.at[here]))
        later.append((part.at[:, pl.ds(half, half)], count_ref.at[here]))
        low += part.shape[0]
    later.append((w_in_hbm.at[pl.ds(0, w_hot_ref.shape[0])], w_hot_ref))
    later.append((pre_hbm.at[pl.ds(0, pre_ref.shape[0])], pre_ref))
    copies = [
        pltpu.make_async_copy(source, target, sems.at[i])
        for i, (source, target) in enumerate(needed + later)
    ]
    for copy in copies:
        copy.start()
    for copy in copies[: len(counts)]:
        copy.wait()

    def step(i, _):
        here = pl.ds(pl.multiple_of(i * TILE, TILE), TILE)
        pool_ref[here, :] = dot(held_ref[here, :], own_ref[...])
        return 0

    lax.fori_loop(0, low // TILE, step, 0)
    for copy in copies[len(counts) :]:
        copy.wait()


def own_pool(counts, fresh_own, pre, w_in):
    half, width = fresh_own.shape
    batch, hidden = pre.shape
    return pl.pallas_call(
        own_kernel,
        out_shape=(
            pltpu.VMEM((batch, width), F32),
            pltpu.VMEM((batch, half), BF16),
            pltpu.VMEM((TILE, hidden), BF16),
            pltpu.VMEM((width, hidden), BF16),
        ),
        in_specs=[VMEM] + [HBM] * (2 + len(counts)),
        out_specs=(VMEM, VMEM, VMEM, VMEM),
        scratch_shapes=[
            pltpu.VMEM((batch, half), BF16), pltpu.SemaphoreType.DMA((2 * len(counts) + 2,))
        ],
        compiler_params=params(16),
        cost_estimate=cost(2 * batch * half * width, 3 * batch * width * 4),
    )(fresh_own, in_hbm(pre), in_hbm(w_in), *(in_hbm(c) for c in counts))


def mlp_kernel(
    pool_ref, count_ref, other_ref, w_hot_ref, first_pre_ref, pre_hbm, w_out_hbm, b_ref, out_hbm,
    hidden_ref, w_out_ref, pre_ref, out_ref, pre_sems, w_sems, out_sems,
):
    tiles = hidden_ref.shape[0] // TILE
    pieces, _, columns = w_out_ref.shape

    def load_pre(i):
        here = pl.ds(pl.multiple_of(i * TILE, TILE), TILE)
        return pltpu.make_async_copy(pre_hbm.at[here], pre_ref.at[i], pre_sems.at[i])

    def load_w(n):
        here = pl.ds(pl.multiple_of(n * columns, columns), columns)
        return pltpu.make_async_copy(w_out_hbm.at[:, here], w_out_ref.at[n], w_sems.at[n])

    def leave(n):
        here = pl.ds(pl.multiple_of(n * columns, columns), columns)
        slot = lax.rem(n, 2)
        return pltpu.make_async_copy(out_ref.at[slot], out_hbm.at[:, here], out_sems.at[slot])

    for i in range(1, tiles):
        load_pre(i).start()
    load_w(0).start()
    pre_ref[0] = first_pre_ref[...]

    def first_layer(i, _):
        here = pl.ds(pl.multiple_of(i * TILE, TILE), TILE)
        pool = pool_ref[here, :] + dot(count_ref[here, :], other_ref[...])

        @pl.when(i > 0)
        def _():
            load_pre(i).wait()

            @pl.when(i < pieces)
            def _():
                load_w(i).start()

        pre = dot(pool.astype(BF16), w_hot_ref[...]) + pre_ref[i].astype(F32)
        hidden_ref[here, :] = jnp.maximum(pre, 0.0).astype(BF16)
        return 0

    lax.fori_loop(0, tiles, first_layer, 0)

    def second_layer(n, _):
        load_w(n).wait()

        @pl.when(n >= 2)
        def _():
            leave(n - 2).wait()

        here = pl.ds(pl.multiple_of(n * columns, columns), columns)
        out_ref[lax.rem(n, 2)] = dot(hidden_ref[...], w_out_ref[n]) + b_ref[:, here]
        leave(n).start()
        return 0

    lax.fori_loop(0, pieces, second_layer, 0)
    leave(pieces - 2).wait()
    leave(pieces - 1).wait()


def mlp(pool, counts, fresh_other, w_hot, first_pre, pre, w_out, b_out):
    batch, hidden = pre.shape
    wide = w_out.shape[1]
    half, width = fresh_other.shape
    pieces = wide // PIECE
    return pl.pallas_call(
        mlp_kernel,
        out_shape=jax.ShapeDtypeStruct((batch, wide), F32),
        in_specs=[VMEM] * 5 + [HBM, HBM, VMEM],
        out_specs=HBM,
        scratch_shapes=[
            pltpu.VMEM((batch, hidden), BF16),
            pltpu.VMEM((pieces, hidden, PIECE), BF16),
            pltpu.VMEM((batch // TILE, TILE, hidden), BF16),
            pltpu.VMEM((2, batch, PIECE), F32),
            pltpu.SemaphoreType.DMA((batch // TILE,)),
            pltpu.SemaphoreType.DMA((pieces,)),
            pltpu.SemaphoreType.DMA((2,)),
        ],
        compiler_params=params(36),
        cost_estimate=cost(
            2 * batch * (half * width + width * hidden + hidden * wide), batch * wide * 4
        ),
    )(
        pool, counts, fresh_other, w_hot, first_pre, in_hbm(pre), in_hbm(w_out),
        b_out.reshape(1, wide),
    )


def on_device(
    hot_grad,
    first_moment,
    second_moment,
    hot_master,
    hot_ids,
    hot_lengths,
    cold_table,
    cold_index,
    cold_count,
    cold_sample,
    w_in,
    b_in,
    w_out,
    b_out,
):
    width = cold_table.shape[1]
    batch = hot_lengths.shape[2]
    hot = hot_grad.shape[2]
    n_dp, n_table = lax.axis_size("dp"), lax.axis_size("table")
    lines = n_table // 2
    own = hot // (n_dp * n_table)
    swap = [(i, i ^ 1) for i in range(n_table)]

    def along(array, step):
        pairs = [(i, (i + 2 * step) % n_table) for i in range(n_table)]
        return lax.ppermute(array, "table", pairs)

    grad = hot_grad[0, 0].reshape(n_dp, lines, 2, own, width)
    send = other_half(grad)
    other = lax.ppermute(send, "table", swap)
    index, counts = cold_index[0, 0], cold_count[0]
    (index_far,) = after(send, index)
    far, mine = pick(index_far, counts, cold_table, grad)
    chip = chip_rows(mine, other)

    parts = lax.all_to_all(
        chip.reshape(n_dp, lines * own, width), "dp", split_axis=0, concat_axis=0, tiled=True
    )
    far_in = lax.ppermute(far, "table", swap)
    (index_near,) = after(chip, index)
    (near,) = pick(index_near, counts, cold_table)
    blocks = merge(near, far_in, lines)
    rows_in = [along(blocks[s], s) if s in (1, lines - 1) else blocks[s] for s in range(lines)]

    ids, lengths = hot_ids[0], hot_lengths[0]
    blocks_in_all = batch // BAGS
    early = blocks_in_all * 3 // 4
    (ids_now,) = after(blocks[0], ids)
    count_low = count_matrix(ids_now, lengths, hot, own, 0, early)
    (parts,) = after(count_low, parts)
    share = sum_parts(parts)
    shares_in = [along(share, s) for s in (1, 3, 2)]
    spread, new_master, new_first, new_second = update(
        share, shares_in, hot_master, first_moment, second_moment, n_dp, lines, own
    )
    fresh_own = lax.all_to_all(spread, "dp", split_axis=0, concat_axis=0, tiled=True)
    samples, ids_late, *further = after(spread, cold_sample[0, 0], ids, *rows_in[2:-1])
    rows_in[2:-1] = [along(block, 2 + s) for s, block in enumerate(further)]
    count_high = count_matrix(ids_late, lengths, hot, own, early, blocks_in_all - early)
    pre = cold_half(samples, rows_in, w_in, b_in, batch)
    fresh_own, *_ = lax.optimization_barrier((fresh_own, pre, count_high))
    fresh_own = fresh_own.reshape(hot // 2, width)
    fresh_other = lax.ppermute(fresh_own, "table", swap)
    pool, counts_other, first_pre, w_hot = own_pool(
        [count_low, count_high], fresh_own, pre, w_in
    )
    fresh_other, pool = lax.optimization_barrier((fresh_other, pool))
    result = mlp(pool, counts_other, fresh_other, w_hot, first_pre, pre, w_out, b_out)
    return (result[None, None], new_master, new_first, new_second)


def solution(mesh):
    return jax.shard_map(
        on_device,
        mesh=mesh,
        in_specs=(
            P("dp", "table", None, None),
            P("dp", None),
            P("dp", None),
            P("dp", None),
            P("dp", "table", None),
            P("dp", "table", None),
            P("table", None),
            P("dp", "table", None, None),
            P("dp", "table", None),
            P("dp", "table", None, None),
            P(),
            P(),
            P(),
            P(),
        ),
        out_specs=(
            P("dp", "table", None, None),
            P(("dp", "table"), None),
            P(("dp", "table"), None),
            P(("dp", "table"), None),
        ),
        check_vma=False,
    )
```

```python
import functools

import jax
import jax.numpy as jnp
from jax import lax
from jax.experimental import pallas as pl
from jax.experimental.pallas import tpu as pltpu
from jax.sharding import PartitionSpec as P

beta_first = 0.9
beta_second = 0.999
adam_count = 10
learning_rate = 0.05
weight_decay = 0.01
epsilon = 1e-08

BF16 = jnp.bfloat16
F32 = jnp.float32
I32 = jnp.int32
I16 = jnp.int16
VMEM = pl.BlockSpec(memory_space=pltpu.VMEM)
HBM = pl.BlockSpec(memory_space=pltpu.HBM)
MIB = 1 << 20
CHUNK = 512
BAGS = 256
LANES = 128
TILE = 256
ROWS = 512
PIECE = 512
LAST = (((1,), (1,)), ((), ()))
FIRST = (((0,), (0,)), ((), ()))


def adamw(master, first, second, grad):
    first_new = beta_first * first + (1.0 - beta_first) * grad
    second_new = beta_second * second + (1.0 - beta_second) * grad * grad
    corrected = first_new / (1.0 - beta_first**adam_count)
    scaled = second_new / (1.0 - beta_second**adam_count)
    master_new = master - learning_rate * (
        corrected / (jnp.sqrt(scaled) + epsilon) + weight_decay * master
    )
    return (master_new, first_new, second_new)


def dot(a, b):
    return jnp.dot(a, b, preferred_element_type=F32)


def dot_on(a, b, dims):
    return lax.dot_general(a, b, dims, preferred_element_type=F32)


def params(mib):
    return pltpu.CompilerParams(vmem_limit_bytes=mib * MIB)


def cost(flops, moved):
    return pl.CostEstimate(flops=flops, bytes_accessed=moved, transcendentals=0)


def in_hbm(array):
    return pltpu.with_memory_space_constraint(array, pltpu.HBM)


def my_place():
    place = lax.axis_index("table")
    return lax.rem(place, 2), lax.div(place, 2)


def after(first, *others):
    return lax.optimization_barrier((first, *others))[1:]


def load_half(grad_ref, side, held_ref, sems):
    steps = sems.shape[0]
    part = grad_ref.shape[0] // steps
    copies = []
    for i in range(steps):
        here = pl.ds(i * part, part)
        copy = pltpu.make_async_copy(
            grad_ref.at[here, :, side], held_ref.at[here], sems.at[i]
        )
        copy.start()
        copies.append(copy)
    return copies


def half_kernel(grad_ref, out_ref, held_ref, sems):
    core, _ = my_place()
    copies = load_half(grad_ref, 1 - core, held_ref, sems)
    rows, part = out_ref.shape[0] // len(copies), held_ref.shape[0] // len(copies)
    for i, copy in enumerate(copies):
        copy.wait()
        mine = held_ref[i * part : (i + 1) * part].reshape(rows, out_ref.shape[1])
        out_ref[i * rows : (i + 1) * rows, :] = mine.astype(BF16)


def other_half(grad):
    n_dp, lines, _, own, width = grad.shape
    total = n_dp * lines * own
    return pl.pallas_call(
        half_kernel,
        out_shape=jax.ShapeDtypeStruct((total, width), BF16),
        in_specs=[HBM],
        out_specs=VMEM,
        scratch_shapes=[
            pltpu.VMEM((n_dp, lines, own, width), F32), pltpu.SemaphoreType.DMA((4,))
        ],
        compiler_params=params(16),
        cost_estimate=cost(0, total * width * 6),
    )(in_hbm(grad))


def chip_kernel(mine_ref, other_ref, out_hbm, out_ref, sems):
    steps = sems.shape[0]
    rows, part = other_ref.shape[0] // steps, mine_ref.shape[0] // steps
    copies = []
    for i in range(steps):
        here = slice(i * rows, (i + 1) * rows)
        mine = mine_ref[i * part : (i + 1) * part].reshape(rows, out_ref.shape[1])
        out_ref[here, :] = (mine + other_ref[here, :].astype(F32)).astype(BF16)
        block = pl.ds(i * rows, rows)
        copy = pltpu.make_async_copy(out_ref.at[block], out_hbm.at[block], sems.at[i])
        copy.start()
        copies.append(copy)
    for copy in copies:
        copy.wait()


def chip_rows(mine, other):
    return pl.pallas_call(
        chip_kernel,
        out_shape=pltpu.HBM(other.shape, BF16),
        in_specs=[VMEM, VMEM],
        out_specs=HBM,
        scratch_shapes=[pltpu.VMEM(other.shape, BF16), pltpu.SemaphoreType.DMA((4,))],
        compiler_params=params(16),
        cost_estimate=cost(0, other.size * 8),
    )(mine, other)


def sum_kernel(parts_ref, out_ref):
    total = parts_ref[0].astype(F32)
    for i in range(1, parts_ref.shape[0]):
        total = total + parts_ref[i].astype(F32)
    out_ref[...] = total


def sum_parts(parts):
    return pl.pallas_call(
        sum_kernel,
        out_shape=jax.ShapeDtypeStruct(parts.shape[1:], F32),
        in_specs=[VMEM],
        out_specs=VMEM,
        compiler_params=params(16),
        cost_estimate=cost(parts.size, parts.size * 2),
    )(parts)


def update_kernel(
    share_ref, in1_ref, in2_ref, in3_ref, master_ref, first_ref, second_ref,
    spread_ref, new_master_ref, new_first_ref, new_second_ref,
):
    core, line = my_place()
    lines, _, own, width = master_ref.shape
    grad = (share_ref[...] + in1_ref[...]) + (in2_ref[...] + in3_ref[...])
    rows = lines * own
    master, first, second = adamw(
        master_ref[:, core].reshape(rows, width),
        first_ref[:, core].reshape(rows, width),
        second_ref[:, core].reshape(rows, width),
        grad,
    )
    fresh = master.astype(BF16)
    for i in range(spread_ref.shape[0]):
        spread_ref[i] = fresh
    for whole, out_ref in (
        (master, new_master_ref), (first, new_first_ref), (second, new_second_ref)
    ):
        picked = whole[:own]
        for i in range(1, lines):
            picked = jnp.where(line == i, whole[i * own : (i + 1) * own], picked)
        out_ref[...] = picked


def update(share, shares_in, master, first, second, n_dp, lines, own):
    width = master.shape[1]
    rows = [a.reshape(lines, 2, own, width) for a in (master, first, second)]
    mine = jax.ShapeDtypeStruct((own, width), F32)
    return pl.pallas_call(
        update_kernel,
        out_shape=(
            jax.ShapeDtypeStruct((n_dp, lines * own, width), BF16), mine, mine, mine,
        ),
        in_specs=[VMEM] * 7,
        out_specs=(VMEM,) * 4,
        compiler_params=params(16),
        cost_estimate=cost(20 * share.size, 60 * share.size),
    )(share, *shares_in, *rows)


def pick_kernel(other_side, index_hbm, count_hbm, table_hbm, *refs):
    if other_side:
        grad_hbm, out_ref, mine_ref, *scratch, grad_sems = refs
    else:
        out_ref, *scratch = refs
    index_ref, count_ref, table_ref, total_ref, sems = scratch
    asked = [
        pltpu.make_async_copy(index_hbm, index_ref, sems.at[0]),
        pltpu.make_async_copy(count_hbm, count_ref, sems.at[1]),
    ]
    pieces = sems.shape[0] - 2
    part = table_ref.shape[0] // pieces
    copies = [
        pltpu.make_async_copy(
            table_hbm.at[pl.ds(i * part, part)], table_ref.at[pl.ds(i * part, part)], sems.at[2 + i]
        )
        for i in range(pieces)
    ]
    for copy in asked + copies:
        copy.start()
    core, line = my_place()
    grads = load_half(grad_hbm, core, mine_ref, grad_sems) if other_side else []
    side = 1 - core if other_side else core
    askers, slots = index_ref.shape
    lines = askers // 2
    slot = lax.broadcasted_iota(I32, (1, slots), 1)
    each = lax.broadcasted_iota(I32, (1, askers), 1)
    for copy in asked:
        copy.wait()
    wanted = []
    for s in range(lines):
        asker = lax.rem(line + s, lines) * 2 + side
        used = jnp.sum(jnp.where(each == asker, count_ref[...], 0), axis=1, keepdims=True)
        wanted.append(jnp.where(slot < used, index_ref[pl.ds(asker, 1), :], -1).astype(I16))
    wanted = jnp.concatenate(wanted, axis=1)
    rows = lax.broadcasted_iota(I16, (part, lines * slots), 0)
    for i, copy in enumerate(copies):
        hit = jnp.where(rows + I16(i * part) == wanted, BF16(1), BF16(0))
        copy.wait()
        found = dot_on(hit, table_ref[i * part : (i + 1) * part, :], FIRST)
        if i > 0:
            found = found + total_ref[...]
        if i < pieces - 1:
            total_ref[...] = found
        else:
            out_ref[...] = found.astype(BF16)
    for copy in grads:
        copy.wait()


def pick(index, counts, table, grad=None):
    width = table.shape[1]
    rows = index.size // 2
    out = [jax.ShapeDtypeStruct((rows, width), BF16)]
    scratch = [
        pltpu.VMEM(index.shape, I32),
        pltpu.VMEM(counts.shape, I32),
        pltpu.VMEM(table.shape, BF16),
        pltpu.VMEM((rows, width), F32),
        pltpu.SemaphoreType.DMA((6,)),
    ]
    operands = [index, counts, table]
    if grad is not None:
        n_dp, lines, _, own, _ = grad.shape
        out.append(jax.ShapeDtypeStruct((n_dp, lines, own, width), F32))
        scratch.append(pltpu.SemaphoreType.DMA((4,)))
        operands.append(grad)
    return pl.pallas_call(
        functools.partial(pick_kernel, grad is not None),
        out_shape=tuple(out),
        in_specs=[HBM] * len(operands),
        out_specs=(VMEM,) * len(out),
        scratch_shapes=scratch,
        compiler_params=params(24),
        cost_estimate=cost(index.size * table.size, table.size * 2),
    )(*(in_hbm(a) for a in operands))


def merge_kernel(near_ref, far_ref, *out_refs):
    slots = near_ref.shape[0] // len(out_refs)
    for s, out_ref in enumerate(out_refs):
        out_ref[:slots, :] = near_ref[s * slots : (s + 1) * slots, :]
        out_ref[slots:, :] = far_ref[s * slots : (s + 1) * slots, :]


def merge(near, far, lines):
    out = jax.ShapeDtypeStruct((2 * near.shape[0] // lines, near.shape[1]), BF16)
    return pl.pallas_call(
        merge_kernel,
        out_shape=(out,) * lines,
        in_specs=[VMEM, VMEM],
        out_specs=(VMEM,) * lines,
        compiler_params=params(16),
        cost_estimate=cost(0, near.size * 8),
    )(near, far)


def cold_kernel(sample_ref, *refs):
    rows_in, rest = refs[:-8], refs[-8:]
    w_hbm, b_ref, pre_hbm, w_ref, feature_ref, held_ref, sem, out_sems = rest
    core, line = my_place()
    lines = len(rows_in)
    batch, width = feature_ref.shape
    copy = pltpu.make_async_copy(w_hbm.at[pl.ds(width, width)], w_ref, sem)
    copy.start()
    samples = []
    for s in range(lines):
        owner = lax.rem(line + lines - s, lines) * 2
        samples.append(
            jnp.concatenate(
                [sample_ref[pl.ds(owner + side, 1), :] for side in (core, 1 - core)], axis=1
            )
        )
    bag = lax.broadcasted_iota(I16, (ROWS, samples[0].shape[1]), 0)

    def pool_step(i, _):
        pool = None
        for sample, rows_ref in zip(samples, rows_in, strict=True):
            hit = bag == (sample - i * ROWS).astype(I16)
            part = dot(jnp.where(hit, BF16(1), BF16(0)), rows_ref[...])
            pool = part if pool is None else pool + part
        feature_ref[pl.ds(pl.multiple_of(i * ROWS, ROWS), ROWS), :] = pool.astype(BF16)
        return 0

    lax.fori_loop(0, batch // ROWS, pool_step, 0)
    copy.wait()

    def leave(i):
        here = pl.ds(pl.multiple_of(i * TILE, TILE), TILE)
        return pltpu.make_async_copy(held_ref.at[here], pre_hbm.at[here], out_sems.at[i])

    def step(i, _):
        here = pl.ds(pl.multiple_of(i * TILE, TILE), TILE)
        held_ref[here, :] = (dot(feature_ref[here, :], w_ref[...]) + b_ref[...]).astype(BF16)
        leave(i).start()
        return 0

    lax.fori_loop(0, batch // TILE, step, 0)
    for i in range(batch // TILE):
        leave(i).wait()


def cold_half(samples, rows_in, w_in, b_in, batch):
    hidden = w_in.shape[1]
    width = rows_in[0].shape[1]
    return pl.pallas_call(
        cold_kernel,
        out_shape=pltpu.HBM((batch, hidden), BF16),
        in_specs=[VMEM] * (len(rows_in) + 1) + [HBM, VMEM],
        out_specs=HBM,
        scratch_shapes=[
            pltpu.VMEM((width, hidden), BF16),
            pltpu.VMEM((batch, width), BF16),
            pltpu.VMEM((batch, hidden), BF16),
            pltpu.SemaphoreType.DMA(()),
            pltpu.SemaphoreType.DMA((batch // TILE,)),
        ],
        compiler_params=params(24),
        cost_estimate=cost(2 * batch * width * (hidden + samples.size), batch * hidden * 2),
    )(samples, *rows_in, in_hbm(w_in), b_in.reshape(1, hidden))


def count_kernel(low_block, own, ids_ref, lengths_ref, out_hbm, total_ref, out_ref, sems):
    core, _ = my_place()
    bags, width = out_ref.shape
    row = lax.broadcasted_iota(I32, (BAGS, BAGS), 0)
    col = lax.broadcasted_iota(I32, (BAGS, BAGS), 1)
    upto = (col <= row).astype(BF16)
    before = (col < row).astype(BF16)
    rows = lax.broadcasted_iota(I16, (width, CHUNK), 0)
    offset = F32(0.0)
    if low_block:
        offset = jnp.sum(lengths_ref[:, : low_block * BAGS].astype(F32))

    def leave(k):
        here = pl.ds(k * BAGS, BAGS)
        return pltpu.make_async_copy(out_ref.at[here], out_hbm.at[here], sems.at[k])

    for k in range(bags // BAGS):
        at = (low_block + k) * BAGS
        lengths = lengths_ref[:, at : at + BAGS].astype(F32)
        spread = jnp.broadcast_to(lengths, (LANES, BAGS)).astype(BF16)
        end = (offset + dot_on(upto, spread, LAST)).astype(I32).astype(I16)
        start = (offset + dot_on(before, spread, LAST)).astype(I32).astype(I16)
        following = offset + jnp.sum(lengths)
        lowest, highest = offset.astype(I32), following.astype(I32)
        offset = following
        total_ref[...] = jnp.zeros_like(total_ref)

        def step(j, _, start=start, end=end):
            here = pl.multiple_of(j * CHUNK, CHUNK)
            ids = ids_ref[:, pl.ds(here, CHUNK)]
            far = lax.div(ids, own) % 2 != core
            places = lax.div(ids, 2 * own) * own + lax.rem(ids, own)
            places = jnp.where(far, places + width // 2, places).astype(I16)
            hits = jnp.where(rows == places, BF16(1), BF16(0))
            lane = (here + lax.broadcasted_iota(I32, (1, CHUNK), 1)).astype(I16)
            parts = []
            for o in range(0, CHUNK, LANES):
                at_lane = lane[:, o : o + LANES]
                inside = (start <= at_lane) & (at_lane < end)
                parts.append(jnp.where(inside, BF16(1), BF16(0)))
            total_ref[...] += dot_on(jnp.concatenate(parts, axis=1), hits, LAST)
            return 0

        lax.fori_loop(lowest // CHUNK, (highest + CHUNK - 1) // CHUNK, step, 0)
        out_ref[k * BAGS : (k + 1) * BAGS, :] = total_ref[...].astype(BF16)
        leave(k).start()
    for k in range(bags // BAGS):
        leave(k).wait()


def count_matrix(ids, lengths, width, own, low_block, blocks):
    return pl.pallas_call(
        functools.partial(count_kernel, low_block, own),
        out_shape=pltpu.HBM((blocks * BAGS, width), BF16),
        in_specs=[VMEM, VMEM],
        out_specs=HBM,
        scratch_shapes=[
            pltpu.VMEM((BAGS, width), F32),
            pltpu.VMEM((blocks * BAGS, width), BF16),
            pltpu.SemaphoreType.DMA((blocks,)),
        ],
        compiler_params=params(24),
        cost_estimate=cost(3 * blocks * 2 * BAGS * CHUNK * width, 2 * blocks * BAGS * width),
    )(ids, lengths)


def own_kernel(own_ref, pre_hbm, w_in_hbm, *refs):
    counts, rest = refs[:-6], refs[-6:]
    pool_ref, count_ref, pre_ref, w_hot_ref, held_ref, sems = rest
    half = own_ref.shape[0]
    needed, later, low = [], [], 0
    for part in counts:
        here = pl.ds(low, part.shape[0])
        needed.append((part.at[:, pl.ds(0, half)], held_ref.at[here]))
        later.append((part.at[:, pl.ds(half, half)], count_ref.at[here]))
        low += part.shape[0]
    later.append((w_in_hbm.at[pl.ds(0, w_hot_ref.shape[0])], w_hot_ref))
    later.append((pre_hbm.at[pl.ds(0, pre_ref.shape[0])], pre_ref))
    copies = [
        pltpu.make_async_copy(source, target, sems.at[i])
        for i, (source, target) in enumerate(needed + later)
    ]
    for copy in copies:
        copy.start()
    for copy in copies[: len(counts)]:
        copy.wait()

    def step(i, _):
        here = pl.ds(pl.multiple_of(i * TILE, TILE), TILE)
        pool_ref[here, :] = dot(held_ref[here, :], own_ref[...])
        return 0

    lax.fori_loop(0, low // TILE, step, 0)
    for copy in copies[len(counts) :]:
        copy.wait()


def own_pool(counts, fresh_own, pre, w_in):
    half, width = fresh_own.shape
    batch, hidden = pre.shape
    return pl.pallas_call(
        own_kernel,
        out_shape=(
            pltpu.VMEM((batch, width), F32),
            pltpu.VMEM((batch, half), BF16),
            pltpu.VMEM((TILE, hidden), BF16),
            pltpu.VMEM((width, hidden), BF16),
        ),
        in_specs=[VMEM] + [HBM] * (2 + len(counts)),
        out_specs=(VMEM, VMEM, VMEM, VMEM),
        scratch_shapes=[
            pltpu.VMEM((batch, half), BF16), pltpu.SemaphoreType.DMA((2 * len(counts) + 2,))
        ],
        compiler_params=params(16),
        cost_estimate=cost(2 * batch * half * width, 3 * batch * width * 4),
    )(fresh_own, in_hbm(pre), in_hbm(w_in), *(in_hbm(c) for c in counts))


def mlp_kernel(
    pool_ref, count_ref, other_ref, w_hot_ref, first_pre_ref, pre_hbm, w_out_hbm, b_ref, out_hbm,
    hidden_ref, w_out_ref, pre_ref, out_ref, pre_sems, w_sems, out_sems,
):
    tiles = hidden_ref.shape[0] // TILE
    pieces, _, columns = w_out_ref.shape

    def load_pre(i):
        here = pl.ds(pl.multiple_of(i * TILE, TILE), TILE)
        return pltpu.make_async_copy(pre_hbm.at[here], pre_ref.at[i], pre_sems.at[i])

    def load_w(n):
        here = pl.ds(pl.multiple_of(n * columns, columns), columns)
        return pltpu.make_async_copy(w_out_hbm.at[:, here], w_out_ref.at[n], w_sems.at[n])

    def leave(n):
        here = pl.ds(pl.multiple_of(n * columns, columns), columns)
        slot = lax.rem(n, 2)
        return pltpu.make_async_copy(out_ref.at[slot], out_hbm.at[:, here], out_sems.at[slot])

    for i in range(1, tiles):
        load_pre(i).start()
    load_w(0).start()
    pre_ref[0] = first_pre_ref[...]

    def first_layer(i, _):
        here = pl.ds(pl.multiple_of(i * TILE, TILE), TILE)
        pool = pool_ref[here, :] + dot(count_ref[here, :], other_ref[...])

        @pl.when(i > 0)
        def _():
            load_pre(i).wait()

            @pl.when(i < pieces)
            def _():
                load_w(i).start()

        pre = dot(pool.astype(BF16), w_hot_ref[...]) + pre_ref[i].astype(F32)
        hidden_ref[here, :] = jnp.maximum(pre, 0.0).astype(BF16)
        return 0

    lax.fori_loop(0, tiles, first_layer, 0)

    def second_layer(n, _):
        load_w(n).wait()

        @pl.when(n >= 2)
        def _():
            leave(n - 2).wait()

        here = pl.ds(pl.multiple_of(n * columns, columns), columns)
        out_ref[lax.rem(n, 2)] = dot(hidden_ref[...], w_out_ref[n]) + b_ref[:, here]
        leave(n).start()
        return 0

    lax.fori_loop(0, pieces, second_layer, 0)
    leave(pieces - 2).wait()
    leave(pieces - 1).wait()


def mlp(pool, counts, fresh_other, w_hot, first_pre, pre, w_out, b_out):
    batch, hidden = pre.shape
    wide = w_out.shape[1]
    half, width = fresh_other.shape
    pieces = wide // PIECE
    return pl.pallas_call(
        mlp_kernel,
        out_shape=jax.ShapeDtypeStruct((batch, wide), F32),
        in_specs=[VMEM] * 5 + [HBM, HBM, VMEM],
        out_specs=HBM,
        scratch_shapes=[
            pltpu.VMEM((batch, hidden), BF16),
            pltpu.VMEM((pieces, hidden, PIECE), BF16),
            pltpu.VMEM((batch // TILE, TILE, hidden), BF16),
            pltpu.VMEM((2, batch, PIECE), F32),
            pltpu.SemaphoreType.DMA((batch // TILE,)),
            pltpu.SemaphoreType.DMA((pieces,)),
            pltpu.SemaphoreType.DMA((2,)),
        ],
        compiler_params=params(36),
        cost_estimate=cost(
            2 * batch * (half * width + width * hidden + hidden * wide), batch * wide * 4
        ),
    )(
        pool, counts, fresh_other, w_hot, first_pre, in_hbm(pre), in_hbm(w_out),
        b_out.reshape(1, wide),
    )


def on_device(
    hot_grad,
    first_moment,
    second_moment,
    hot_master,
    hot_ids,
    hot_lengths,
    cold_table,
    cold_index,
    cold_count,
    cold_sample,
    w_in,
    b_in,
    w_out,
    b_out,
):
    width = cold_table.shape[1]
    batch = hot_lengths.shape[2]
    hot = hot_grad.shape[2]
    n_dp, n_table = lax.axis_size("dp"), lax.axis_size("table")
    lines = n_table // 2
    own = hot // (n_dp * n_table)
    swap = [(i, i ^ 1) for i in range(n_table)]

    def along(array, step):
        pairs = [(i, (i + 2 * step) % n_table) for i in range(n_table)]
        return lax.ppermute(array, "table", pairs)

    grad = hot_grad[0, 0].reshape(n_dp, lines, 2, own, width)
    send = other_half(grad)
    other = lax.ppermute(send, "table", swap)
    index, counts = cold_index[0, 0], cold_count[0]
    (index_far,) = after(send, index)
    far, mine = pick(index_far, counts, cold_table, grad)
    chip = chip_rows(mine, other)

    parts = lax.all_to_all(
        chip.reshape(n_dp, lines * own, width), "dp", split_axis=0, concat_axis=0, tiled=True
    )
    far_in = lax.ppermute(far, "table", swap)
    (index_near,) = after(chip, index)
    (near,) = pick(index_near, counts, cold_table)
    blocks = merge(near, far_in, lines)
    rows_in = [along(blocks[s], s) if s in (1, lines - 1) else blocks[s] for s in range(lines)]

    ids, lengths = hot_ids[0], hot_lengths[0]
    blocks_in_all = batch // BAGS
    early = blocks_in_all // 2
    (ids_now,) = after(blocks[0], ids)
    count_low = count_matrix(ids_now, lengths, hot, own, 0, early)
    (parts,) = after(count_low, parts)
    share = sum_parts(parts)
    shares_in = [along(share, s) for s in (1, 3, 2)]
    spread, new_master, new_first, new_second = update(
        share, shares_in, hot_master, first_moment, second_moment, n_dp, lines, own
    )
    fresh_own = lax.all_to_all(spread, "dp", split_axis=0, concat_axis=0, tiled=True)
    samples, ids_late, *further = after(spread, cold_sample[0, 0], ids, *rows_in[2:-1])
    rows_in[2:-1] = [along(block, 2 + s) for s, block in enumerate(further)]
    count_high = count_matrix(ids_late, lengths, hot, own, early, blocks_in_all - early)
    pre = cold_half(samples, rows_in, w_in, b_in, batch)
    fresh_own, *_ = lax.optimization_barrier((fresh_own, pre, count_high))
    fresh_own = fresh_own.reshape(hot // 2, width)
    fresh_other = lax.ppermute(fresh_own, "table", swap)
    pool, counts_other, first_pre, w_hot = own_pool(
        [count_low, count_high], fresh_own, pre, w_in
    )
    fresh_other, pool = lax.optimization_barrier((fresh_other, pool))
    result = mlp(pool, counts_other, fresh_other, w_hot, first_pre, pre, w_out, b_out)
    return (result[None, None], new_master, new_first, new_second)


def solution(mesh):
    return jax.shard_map(
        on_device,
        mesh=mesh,
        in_specs=(
            P("dp", "table", None, None),
            P("dp", None),
            P("dp", None),
            P("dp", None),
            P("dp", "table", None),
            P("dp", "table", None),
            P("table", None),
            P("dp", "table", None, None),
            P("dp", "table", None),
            P("dp", "table", None, None),
            P(),
            P(),
            P(),
            P(),
        ),
        out_specs=(
            P("dp", "table", None, None),
            P(("dp", "table"), None),
            P(("dp", "table"), None),
            P(("dp", "table"), None),
        ),
        check_vma=False,
    )
```

```python
import functools

import jax
import jax.numpy as jnp
from jax import lax
from jax.experimental import pallas as pl
from jax.experimental.pallas import tpu as pltpu
from jax.sharding import PartitionSpec as P

beta_first = 0.9
beta_second = 0.999
adam_count = 10
learning_rate = 0.05
weight_decay = 0.01
epsilon = 1e-08

BF16 = jnp.bfloat16
F32 = jnp.float32
I32 = jnp.int32
I16 = jnp.int16
VMEM = pl.BlockSpec(memory_space=pltpu.VMEM)
HBM = pl.BlockSpec(memory_space=pltpu.HBM)
MIB = 1 << 20
CHUNK = 512
BAGS = 256
LANES = 128
TILE = 256
ROWS = 512
PIECE = 512
LAST = (((1,), (1,)), ((), ()))
FIRST = (((0,), (0,)), ((), ()))


def adamw(master, first, second, grad):
    first_new = beta_first * first + (1.0 - beta_first) * grad
    second_new = beta_second * second + (1.0 - beta_second) * grad * grad
    corrected = first_new / (1.0 - beta_first**adam_count)
    scaled = second_new / (1.0 - beta_second**adam_count)
    master_new = master - learning_rate * (
        corrected / (jnp.sqrt(scaled) + epsilon) + weight_decay * master
    )
    return (master_new, first_new, second_new)


def dot(a, b):
    return jnp.dot(a, b, preferred_element_type=F32)


def dot_on(a, b, dims):
    return lax.dot_general(a, b, dims, preferred_element_type=F32)


def params(mib):
    return pltpu.CompilerParams(vmem_limit_bytes=mib * MIB)


def cost(flops, moved):
    return pl.CostEstimate(flops=flops, bytes_accessed=moved, transcendentals=0)


def in_hbm(array):
    return pltpu.with_memory_space_constraint(array, pltpu.HBM)


def my_place():
    place = lax.axis_index("table")
    return lax.rem(place, 2), lax.div(place, 2)


def after(first, *others):
    return lax.optimization_barrier((first, *others))[1:]


def load_half(grad_ref, side, held_ref, sems):
    steps = sems.shape[0]
    part = grad_ref.shape[0] // steps
    copies = []
    for i in range(steps):
        here = pl.ds(i * part, part)
        copy = pltpu.make_async_copy(
            grad_ref.at[here, :, side], held_ref.at[here], sems.at[i]
        )
        copy.start()
        copies.append(copy)
    return copies


def half_kernel(grad_ref, out_ref, held_ref, sems):
    core, _ = my_place()
    copies = load_half(grad_ref, 1 - core, held_ref, sems)
    rows, part = out_ref.shape[0] // len(copies), held_ref.shape[0] // len(copies)
    for i, copy in enumerate(copies):
        copy.wait()
        mine = held_ref[i * part : (i + 1) * part].reshape(rows, out_ref.shape[1])
        out_ref[i * rows : (i + 1) * rows, :] = mine.astype(BF16)


def other_half(grad):
    n_dp, lines, _, own, width = grad.shape
    total = n_dp * lines * own
    return pl.pallas_call(
        half_kernel,
        out_shape=jax.ShapeDtypeStruct((total, width), BF16),
        in_specs=[HBM],
        out_specs=VMEM,
        scratch_shapes=[
            pltpu.VMEM((n_dp, lines, own, width), F32), pltpu.SemaphoreType.DMA((4,))
        ],
        compiler_params=params(16),
        cost_estimate=cost(0, total * width * 6),
    )(in_hbm(grad))


def chip_kernel(mine_ref, other_ref, out_hbm, out_ref, sems):
    steps = sems.shape[0]
    rows, part = other_ref.shape[0] // steps, mine_ref.shape[0] // steps
    copies = []
    for i in range(steps):
        here = slice(i * rows, (i + 1) * rows)
        mine = mine_ref[i * part : (i + 1) * part].reshape(rows, out_ref.shape[1])
        out_ref[here, :] = (mine + other_ref[here, :].astype(F32)).astype(BF16)
        block = pl.ds(i * rows, rows)
        copy = pltpu.make_async_copy(out_ref.at[block], out_hbm.at[block], sems.at[i])
        copy.start()
        copies.append(copy)
    for copy in copies:
        copy.wait()


def chip_rows(mine, other):
    return pl.pallas_call(
        chip_kernel,
        out_shape=pltpu.HBM(other.shape, BF16),
        in_specs=[VMEM, VMEM],
        out_specs=HBM,
        scratch_shapes=[pltpu.VMEM(other.shape, BF16), pltpu.SemaphoreType.DMA((4,))],
        compiler_params=params(16),
        cost_estimate=cost(0, other.size * 8),
    )(mine, other)


def sum_kernel(parts_ref, out_ref):
    total = parts_ref[0].astype(F32)
    for i in range(1, parts_ref.shape[0]):
        total = total + parts_ref[i].astype(F32)
    out_ref[...] = total


def sum_parts(parts):
    return pl.pallas_call(
        sum_kernel,
        out_shape=jax.ShapeDtypeStruct(parts.shape[1:], F32),
        in_specs=[VMEM],
        out_specs=VMEM,
        compiler_params=params(16),
        cost_estimate=cost(parts.size, parts.size * 2),
    )(parts)


def update_kernel(
    share_ref, in1_ref, in2_ref, in3_ref, master_ref, first_ref, second_ref,
    spread_ref, new_master_ref, new_first_ref, new_second_ref,
):
    core, line = my_place()
    lines, _, own, width = master_ref.shape
    grad = (share_ref[...] + in1_ref[...]) + (in2_ref[...] + in3_ref[...])
    rows = lines * own
    master, first, second = adamw(
        master_ref[:, core].reshape(rows, width),
        first_ref[:, core].reshape(rows, width),
        second_ref[:, core].reshape(rows, width),
        grad,
    )
    fresh = master.astype(BF16)
    for i in range(spread_ref.shape[0]):
        spread_ref[i] = fresh
    for whole, out_ref in (
        (master, new_master_ref), (first, new_first_ref), (second, new_second_ref)
    ):
        picked = whole[:own]
        for i in range(1, lines):
            picked = jnp.where(line == i, whole[i * own : (i + 1) * own], picked)
        out_ref[...] = picked


def update(share, shares_in, master, first, second, n_dp, lines, own):
    width = master.shape[1]
    rows = [a.reshape(lines, 2, own, width) for a in (master, first, second)]
    mine = jax.ShapeDtypeStruct((own, width), F32)
    return pl.pallas_call(
        update_kernel,
        out_shape=(
            jax.ShapeDtypeStruct((n_dp, lines * own, width), BF16), mine, mine, mine,
        ),
        in_specs=[VMEM] * 7,
        out_specs=(VMEM,) * 4,
        compiler_params=params(16),
        cost_estimate=cost(20 * share.size, 60 * share.size),
    )(share, *shares_in, *rows)


def pick_kernel(other_side, index_hbm, count_hbm, table_hbm, *refs):
    if other_side:
        grad_hbm, out_ref, mine_ref, *scratch, grad_sems = refs
    else:
        out_ref, *scratch = refs
    index_ref, count_ref, table_ref, total_ref, sems = scratch
    asked = [
        pltpu.make_async_copy(index_hbm, index_ref, sems.at[0]),
        pltpu.make_async_copy(count_hbm, count_ref, sems.at[1]),
    ]
    pieces = sems.shape[0] - 2
    part = table_ref.shape[0] // pieces
    copies = [
        pltpu.make_async_copy(
            table_hbm.at[pl.ds(i * part, part)], table_ref.at[pl.ds(i * part, part)], sems.at[2 + i]
        )
        for i in range(pieces)
    ]
    for copy in asked + copies:
        copy.start()
    core, line = my_place()
    grads = load_half(grad_hbm, core, mine_ref, grad_sems) if other_side else []
    side = 1 - core if other_side else core
    askers, slots = index_ref.shape
    lines = askers // 2
    slot = lax.broadcasted_iota(I32, (1, slots), 1)
    each = lax.broadcasted_iota(I32, (1, askers), 1)
    for copy in asked:
        copy.wait()
    wanted = []
    for s in range(lines):
        asker = lax.rem(line + s, lines) * 2 + side
        used = jnp.sum(jnp.where(each == asker, count_ref[...], 0), axis=1, keepdims=True)
        wanted.append(jnp.where(slot < used, index_ref[pl.ds(asker, 1), :], -1).astype(I16))
    wanted = jnp.concatenate(wanted, axis=1)
    rows = lax.broadcasted_iota(I16, (part, lines * slots), 0)
    for i, copy in enumerate(copies):
        hit = jnp.where(rows + I16(i * part) == wanted, BF16(1), BF16(0))
        copy.wait()
        found = dot_on(hit, table_ref[i * part : (i + 1) * part, :], FIRST)
        if i > 0:
            found = found + total_ref[...]
        if i < pieces - 1:
            total_ref[...] = found
        else:
            out_ref[...] = found.astype(BF16)
    for copy in grads:
        copy.wait()


def pick(index, counts, table, grad=None):
    width = table.shape[1]
    rows = index.size // 2
    out = [jax.ShapeDtypeStruct((rows, width), BF16)]
    scratch = [
        pltpu.VMEM(index.shape, I32),
        pltpu.VMEM(counts.shape, I32),
        pltpu.VMEM(table.shape, BF16),
        pltpu.VMEM((rows, width), F32),
        pltpu.SemaphoreType.DMA((6,)),
    ]
    operands = [index, counts, table]
    if grad is not None:
        n_dp, lines, _, own, _ = grad.shape
        out.append(jax.ShapeDtypeStruct((n_dp, lines, own, width), F32))
        scratch.append(pltpu.SemaphoreType.DMA((4,)))
        operands.append(grad)
    return pl.pallas_call(
        functools.partial(pick_kernel, grad is not None),
        out_shape=tuple(out),
        in_specs=[HBM] * len(operands),
        out_specs=(VMEM,) * len(out),
        scratch_shapes=scratch,
        compiler_params=params(24),
        cost_estimate=cost(index.size * table.size, table.size * 2),
    )(*(in_hbm(a) for a in operands))


def merge_kernel(near_ref, far_ref, *out_refs):
    slots = near_ref.shape[0] // len(out_refs)
    for s, out_ref in enumerate(out_refs):
        out_ref[:slots, :] = near_ref[s * slots : (s + 1) * slots, :]
        out_ref[slots:, :] = far_ref[s * slots : (s + 1) * slots, :]


def merge(near, far, lines):
    out = jax.ShapeDtypeStruct((2 * near.shape[0] // lines, near.shape[1]), BF16)
    return pl.pallas_call(
        merge_kernel,
        out_shape=(out,) * lines,
        in_specs=[VMEM, VMEM],
        out_specs=(VMEM,) * lines,
        compiler_params=params(16),
        cost_estimate=cost(0, near.size * 8),
    )(near, far)


def cold_kernel(sample_ref, *refs):
    rows_in, rest = refs[:-9], refs[-9:]
    w_hbm, b_ref, pre_hbm, first_ref, w_ref, feature_ref, held_ref, sem, out_sems = rest
    core, line = my_place()
    lines = len(rows_in)
    batch, width = feature_ref.shape
    copy = pltpu.make_async_copy(w_hbm.at[pl.ds(width, width)], w_ref, sem)
    copy.start()
    samples = []
    for s in range(lines):
        owner = lax.rem(line + lines - s, lines) * 2
        samples.append(
            jnp.concatenate(
                [sample_ref[pl.ds(owner + side, 1), :] for side in (core, 1 - core)], axis=1
            )
        )
    bag = lax.broadcasted_iota(I16, (ROWS, samples[0].shape[1]), 0)

    def pool_step(i, _):
        pool = None
        for sample, rows_ref in zip(samples, rows_in, strict=True):
            hit = bag == (sample - i * ROWS).astype(I16)
            part = dot(jnp.where(hit, BF16(1), BF16(0)), rows_ref[...])
            pool = part if pool is None else pool + part
        feature_ref[pl.ds(pl.multiple_of(i * ROWS, ROWS), ROWS), :] = pool.astype(BF16)
        return 0

    lax.fori_loop(0, batch // ROWS, pool_step, 0)
    copy.wait()

    def leave(i):
        here = pl.ds(pl.multiple_of(i * TILE, TILE), TILE)
        return pltpu.make_async_copy(held_ref.at[here], pre_hbm.at[here], out_sems.at[i])

    def step(i, _):
        here = pl.ds(pl.multiple_of(i * TILE, TILE), TILE)
        held_ref[here, :] = (dot(feature_ref[here, :], w_ref[...]) + b_ref[...]).astype(BF16)
        leave(i).start()
        return 0

    lax.fori_loop(0, batch // TILE, step, 0)
    first_ref[...] = held_ref[:TILE, :]
    for i in range(batch // TILE):
        leave(i).wait()


def cold_half(samples, rows_in, w_in, b_in, batch):
    hidden = w_in.shape[1]
    width = rows_in[0].shape[1]
    return pl.pallas_call(
        cold_kernel,
        out_shape=(pltpu.HBM((batch, hidden), BF16), jax.ShapeDtypeStruct((TILE, hidden), BF16)),
        in_specs=[VMEM] * (len(rows_in) + 1) + [HBM, VMEM],
        out_specs=(HBM, VMEM),
        scratch_shapes=[
            pltpu.VMEM((width, hidden), BF16),
            pltpu.VMEM((batch, width), BF16),
            pltpu.VMEM((batch, hidden), BF16),
            pltpu.SemaphoreType.DMA(()),
            pltpu.SemaphoreType.DMA((batch // TILE,)),
        ],
        compiler_params=params(24),
        cost_estimate=cost(2 * batch * width * (hidden + samples.size), batch * hidden * 2),
    )(samples, *rows_in, in_hbm(w_in), b_in.reshape(1, hidden))


def count_kernel(low_block, own, ids_ref, lengths_ref, out_hbm, total_ref, out_ref, sems):
    core, _ = my_place()
    bags, width = out_ref.shape
    row = lax.broadcasted_iota(I32, (BAGS, BAGS), 0)
    col = lax.broadcasted_iota(I32, (BAGS, BAGS), 1)
    upto = (col <= row).astype(BF16)
    before = (col < row).astype(BF16)
    rows = lax.broadcasted_iota(I16, (width, CHUNK), 0)
    offset = F32(0.0)
    if low_block:
        offset = jnp.sum(lengths_ref[:, : low_block * BAGS].astype(F32))

    def leave(k):
        here = pl.ds(k * BAGS, BAGS)
        return pltpu.make_async_copy(out_ref.at[here], out_hbm.at[here], sems.at[k])

    for k in range(bags // BAGS):
        at = (low_block + k) * BAGS
        lengths = lengths_ref[:, at : at + BAGS].astype(F32)
        spread = jnp.broadcast_to(lengths, (LANES, BAGS)).astype(BF16)
        end = (offset + dot_on(upto, spread, LAST)).astype(I32).astype(I16)
        start = (offset + dot_on(before, spread, LAST)).astype(I32).astype(I16)
        following = offset + jnp.sum(lengths)
        lowest, highest = offset.astype(I32), following.astype(I32)
        offset = following
        total_ref[...] = jnp.zeros_like(total_ref)

        def step(j, _, start=start, end=end):
            here = pl.multiple_of(j * CHUNK, CHUNK)
            ids = ids_ref[:, pl.ds(here, CHUNK)]
            far = lax.div(ids, own) % 2 != core
            places = lax.div(ids, 2 * own) * own + lax.rem(ids, own)
            places = jnp.where(far, places + width // 2, places).astype(I16)
            hits = jnp.where(rows == places, BF16(1), BF16(0))
            lane = (here + lax.broadcasted_iota(I32, (1, CHUNK), 1)).astype(I16)
            parts = []
            for o in range(0, CHUNK, LANES):
                at_lane = lane[:, o : o + LANES]
                inside = (start <= at_lane) & (at_lane < end)
                parts.append(jnp.where(inside, BF16(1), BF16(0)))
            total_ref[...] += dot_on(jnp.concatenate(parts, axis=1), hits, LAST)
            return 0

        lax.fori_loop(lowest // CHUNK, (highest + CHUNK - 1) // CHUNK, step, 0)
        out_ref[k * BAGS : (k + 1) * BAGS, :] = total_ref[...].astype(BF16)
        leave(k).start()
    for k in range(bags // BAGS):
        leave(k).wait()


def count_matrix(ids, lengths, width, own, low_block, blocks):
    return pl.pallas_call(
        functools.partial(count_kernel, low_block, own),
        out_shape=pltpu.HBM((blocks * BAGS, width), BF16),
        in_specs=[VMEM, VMEM],
        out_specs=HBM,
        scratch_shapes=[
            pltpu.VMEM((BAGS, width), F32),
            pltpu.VMEM((blocks * BAGS, width), BF16),
            pltpu.SemaphoreType.DMA((blocks,)),
        ],
        compiler_params=params(24),
        cost_estimate=cost(3 * blocks * 2 * BAGS * CHUNK * width, 2 * blocks * BAGS * width),
    )(ids, lengths)


def own_kernel(own_ref, w_in_hbm, *refs):
    counts, rest = refs[:-5], refs[-5:]
    pool_ref, count_ref, w_hot_ref, held_ref, sems = rest
    half = own_ref.shape[0]
    needed, later, low = [], [], 0
    for part in counts:
        here = pl.ds(low, part.shape[0])
        needed.append((part.at[:, pl.ds(0, half)], held_ref.at[here]))
        later.append((part.at[:, pl.ds(half, half)], count_ref.at[here]))
        low += part.shape[0]
    later.append((w_in_hbm.at[pl.ds(0, w_hot_ref.shape[0])], w_hot_ref))
    copies = [
        pltpu.make_async_copy(source, target, sems.at[i])
        for i, (source, target) in enumerate(needed + later)
    ]
    for copy in copies:
        copy.start()
    for copy in copies[: len(counts)]:
        copy.wait()

    def step(i, _):
        here = pl.ds(pl.multiple_of(i * TILE, TILE), TILE)
        pool_ref[here, :] = dot(held_ref[here, :], own_ref[...])
        return 0

    lax.fori_loop(0, low // TILE, step, 0)
    for copy in copies[len(counts) :]:
        copy.wait()


def own_pool(counts, fresh_own, w_in):
    half, width = fresh_own.shape
    batch, hidden = sum(c.shape[0] for c in counts), w_in.shape[1]
    return pl.pallas_call(
        own_kernel,
        out_shape=(
            pltpu.VMEM((batch, width), F32),
            pltpu.VMEM((batch, half), BF16),
            pltpu.VMEM((width, hidden), BF16),
        ),
        in_specs=[VMEM] + [HBM] * (1 + len(counts)),
        out_specs=(VMEM, VMEM, VMEM),
        scratch_shapes=[
            pltpu.VMEM((batch, half), BF16), pltpu.SemaphoreType.DMA((2 * len(counts) + 1,))
        ],
        compiler_params=params(16),
        cost_estimate=cost(2 * batch * half * width, 3 * batch * width * 4),
    )(fresh_own, in_hbm(w_in), *(in_hbm(c) for c in counts))


def mlp_kernel(
    pool_ref, count_ref, other_ref, w_hot_ref, first_pre_ref, pre_hbm, w_out_hbm, b_ref, out_hbm,
    hidden_ref, w_out_ref, pre_ref, out_ref, pre_sems, w_sems, out_sems,
):
    tiles = hidden_ref.shape[0] // TILE
    pieces, _, columns = w_out_ref.shape

    def load_pre(i):
        here = pl.ds(pl.multiple_of(i * TILE, TILE), TILE)
        return pltpu.make_async_copy(pre_hbm.at[here], pre_ref.at[i], pre_sems.at[i])

    def load_w(n):
        here = pl.ds(pl.multiple_of(n * columns, columns), columns)
        return pltpu.make_async_copy(w_out_hbm.at[:, here], w_out_ref.at[n], w_sems.at[n])

    def leave(n):
        here = pl.ds(pl.multiple_of(n * columns, columns), columns)
        slot = lax.rem(n, 2)
        return pltpu.make_async_copy(out_ref.at[slot], out_hbm.at[:, here], out_sems.at[slot])

    for i in range(1, tiles):
        load_pre(i).start()
    load_w(0).start()
    pre_ref[0] = first_pre_ref[...]

    def first_layer(i, _):
        here = pl.ds(pl.multiple_of(i * TILE, TILE), TILE)
        pool = pool_ref[here, :] + dot(count_ref[here, :], other_ref[...])

        @pl.when(i > 0)
        def _():
            load_pre(i).wait()

            @pl.when(i < pieces)
            def _():
                load_w(i).start()

        feature = pool.astype(BF16)
        for low in range(0, w_hot_ref.shape[1], PIECE):
            piece = slice(low, low + PIECE)
            pre = dot(feature, w_hot_ref[:, piece]) + pre_ref[i, :, piece].astype(F32)
            hidden_ref[here, piece] = jnp.maximum(pre, 0.0).astype(BF16)
        return 0

    lax.fori_loop(0, tiles, first_layer, 0)

    def second_layer(n, _):
        load_w(n).wait()

        @pl.when(n >= 2)
        def _():
            leave(n - 2).wait()

        here = pl.ds(pl.multiple_of(n * columns, columns), columns)
        slot = lax.rem(n, 2)
        for low in range(0, hidden_ref.shape[0], TILE):
            rows = slice(low, low + TILE)
            out_ref[slot, rows, :] = dot(hidden_ref[rows, :], w_out_ref[n]) + b_ref[:, here]
        leave(n).start()
        return 0

    lax.fori_loop(0, pieces, second_layer, 0)
    leave(pieces - 2).wait()
    leave(pieces - 1).wait()


def mlp(pool, counts, fresh_other, w_hot, first_pre, pre, w_out, b_out):
    batch, hidden = pre.shape
    wide = w_out.shape[1]
    half, width = fresh_other.shape
    pieces = wide // PIECE
    return pl.pallas_call(
        mlp_kernel,
        out_shape=jax.ShapeDtypeStruct((batch, wide), F32),
        in_specs=[VMEM] * 5 + [HBM, HBM, VMEM],
        out_specs=HBM,
        scratch_shapes=[
            pltpu.VMEM((batch, hidden), BF16),
            pltpu.VMEM((pieces, hidden, PIECE), BF16),
            pltpu.VMEM((batch // TILE, TILE, hidden), BF16),
            pltpu.VMEM((2, batch, PIECE), F32),
            pltpu.SemaphoreType.DMA((batch // TILE,)),
            pltpu.SemaphoreType.DMA((pieces,)),
            pltpu.SemaphoreType.DMA((2,)),
        ],
        compiler_params=params(36),
        cost_estimate=cost(
            2 * batch * (half * width + width * hidden + hidden * wide), batch * wide * 4
        ),
    )(
        pool, counts, fresh_other, w_hot, first_pre, in_hbm(pre), in_hbm(w_out),
        b_out.reshape(1, wide),
    )


def on_device(
    hot_grad,
    first_moment,
    second_moment,
    hot_master,
    hot_ids,
    hot_lengths,
    cold_table,
    cold_index,
    cold_count,
    cold_sample,
    w_in,
    b_in,
    w_out,
    b_out,
):
    width = cold_table.shape[1]
    batch = hot_lengths.shape[2]
    hot = hot_grad.shape[2]
    n_dp, n_table = lax.axis_size("dp"), lax.axis_size("table")
    lines = n_table // 2
    own = hot // (n_dp * n_table)
    swap = [(i, i ^ 1) for i in range(n_table)]

    def along(array, step):
        pairs = [(i, (i + 2 * step) % n_table) for i in range(n_table)]
        return lax.ppermute(array, "table", pairs)

    grad = hot_grad[0, 0].reshape(n_dp, lines, 2, own, width)
    send = other_half(grad)
    other = lax.ppermute(send, "table", swap)
    index, counts = cold_index[0, 0], cold_count[0]
    (index_far,) = after(send, index)
    far, mine = pick(index_far, counts, cold_table, grad)
    chip = chip_rows(mine, other)

    parts = lax.all_to_all(
        chip.reshape(n_dp, lines * own, width), "dp", split_axis=0, concat_axis=0, tiled=True
    )
    far_in = lax.ppermute(far, "table", swap)
    (index_near,) = after(chip, index)
    (near,) = pick(index_near, counts, cold_table)
    blocks = merge(near, far_in, lines)
    rows_in = [along(blocks[s], s) if s in (1, lines - 1) else blocks[s] for s in range(lines)]

    ids, lengths = hot_ids[0], hot_lengths[0]
    blocks_in_all = batch // BAGS
    early = blocks_in_all // 2
    (ids_now,) = after(blocks[0], ids)
    count_low = count_matrix(ids_now, lengths, hot, own, 0, early)
    (parts,) = after(count_low, parts)
    share = sum_parts(parts)
    shares_in = [along(share, s) for s in (1, 3, 2)]
    spread, new_master, new_first, new_second = update(
        share, shares_in, hot_master, first_moment, second_moment, n_dp, lines, own
    )
    fresh_own = lax.all_to_all(spread, "dp", split_axis=0, concat_axis=0, tiled=True)
    samples, ids_late, *further = after(spread, cold_sample[0, 0], ids, *rows_in[2:-1])
    rows_in[2:-1] = [along(block, 2 + s) for s, block in enumerate(further)]
    count_high = count_matrix(ids_late, lengths, hot, own, early, blocks_in_all - early)
    pre, first_pre = cold_half(samples, rows_in, w_in, b_in, batch)
    fresh_own, *_ = lax.optimization_barrier((fresh_own, pre, count_high))
    fresh_own = fresh_own.reshape(hot // 2, width)
    fresh_other = lax.ppermute(fresh_own, "table", swap)
    pool, counts_other, w_hot = own_pool([count_low, count_high], fresh_own, w_in)
    fresh_other, pool = lax.optimization_barrier((fresh_other, pool))
    result = mlp(pool, counts_other, fresh_other, w_hot, first_pre, pre, w_out, b_out)
    return (result[None, None], new_master, new_first, new_second)


def solution(mesh):
    return jax.shard_map(
        on_device,
        mesh=mesh,
        in_specs=(
            P("dp", "table", None, None),
            P("dp", None),
            P("dp", None),
            P("dp", None),
            P("dp", "table", None),
            P("dp", "table", None),
            P("table", None),
            P("dp", "table", None, None),
            P("dp", "table", None),
            P("dp", "table", None, None),
            P(),
            P(),
            P(),
            P(),
        ),
        out_specs=(
            P("dp", "table", None, None),
            P(("dp", "table"), None),
            P(("dp", "table"), None),
            P(("dp", "table"), None),
        ),
        check_vma=False,
    )
```

```python
import functools

import jax
import jax.numpy as jnp
from jax import lax
from jax.experimental import pallas as pl
from jax.experimental.pallas import tpu as pltpu
from jax.sharding import PartitionSpec as P

beta_first = 0.9
beta_second = 0.999
adam_count = 10
learning_rate = 0.05
weight_decay = 0.01
epsilon = 1e-08

BF16 = jnp.bfloat16
F32 = jnp.float32
I32 = jnp.int32
I16 = jnp.int16
VMEM = pl.BlockSpec(memory_space=pltpu.VMEM)
HBM = pl.BlockSpec(memory_space=pltpu.HBM)
MIB = 1 << 20
CHUNK = 512
BAGS = 256
LANES = 128
TILE = 256
ROWS = 512
PIECE = 512
LAST = (((1,), (1,)), ((), ()))
FIRST = (((0,), (0,)), ((), ()))


def adamw(master, first, second, grad):
    first_new = beta_first * first + (1.0 - beta_first) * grad
    second_new = beta_second * second + (1.0 - beta_second) * grad * grad
    corrected = first_new / (1.0 - beta_first**adam_count)
    scaled = second_new / (1.0 - beta_second**adam_count)
    master_new = master - learning_rate * (
        corrected / (jnp.sqrt(scaled) + epsilon) + weight_decay * master
    )
    return (master_new, first_new, second_new)


def dot(a, b):
    return jnp.dot(a, b, preferred_element_type=F32)


def dot_on(a, b, dims):
    return lax.dot_general(a, b, dims, preferred_element_type=F32)


def params(mib):
    return pltpu.CompilerParams(vmem_limit_bytes=mib * MIB)


def cost(flops, moved):
    return pl.CostEstimate(flops=flops, bytes_accessed=moved, transcendentals=0)


def in_hbm(array):
    return pltpu.with_memory_space_constraint(array, pltpu.HBM)


def my_place():
    place = lax.axis_index("table")
    return lax.rem(place, 2), lax.div(place, 2)


def after(first, *others):
    return lax.optimization_barrier((first, *others))[1:]


def load_half(grad_ref, side, held_ref, sems):
    steps = sems.shape[0]
    part = grad_ref.shape[0] // steps
    copies = []
    for i in range(steps):
        here = pl.ds(i * part, part)
        copy = pltpu.make_async_copy(
            grad_ref.at[here, :, side], held_ref.at[here], sems.at[i]
        )
        copy.start()
        copies.append(copy)
    return copies


def half_kernel(grad_ref, out_ref, held_ref, sems):
    core, _ = my_place()
    copies = load_half(grad_ref, 1 - core, held_ref, sems)
    rows, part = out_ref.shape[0] // len(copies), held_ref.shape[0] // len(copies)
    for i, copy in enumerate(copies):
        copy.wait()
        mine = held_ref[i * part : (i + 1) * part].reshape(rows, out_ref.shape[1])
        out_ref[i * rows : (i + 1) * rows, :] = mine.astype(BF16)


def other_half(grad):
    n_dp, lines, _, own, width = grad.shape
    total = n_dp * lines * own
    return pl.pallas_call(
        half_kernel,
        out_shape=jax.ShapeDtypeStruct((total, width), BF16),
        in_specs=[HBM],
        out_specs=VMEM,
        scratch_shapes=[
            pltpu.VMEM((n_dp, lines, own, width), F32), pltpu.SemaphoreType.DMA((4,))
        ],
        compiler_params=params(16),
        cost_estimate=cost(0, total * width * 6),
    )(in_hbm(grad))


def chip_kernel(mine_ref, other_ref, out_hbm, out_ref, sems):
    steps = sems.shape[0]
    rows, part = other_ref.shape[0] // steps, mine_ref.shape[0] // steps
    copies = []
    for i in range(steps):
        here = slice(i * rows, (i + 1) * rows)
        mine = mine_ref[i * part : (i + 1) * part].reshape(rows, out_ref.shape[1])
        out_ref[here, :] = (mine + other_ref[here, :].astype(F32)).astype(BF16)
        block = pl.ds(i * rows, rows)
        copy = pltpu.make_async_copy(out_ref.at[block], out_hbm.at[block], sems.at[i])
        copy.start()
        copies.append(copy)
    for copy in copies:
        copy.wait()


def chip_rows(mine, other):
    return pl.pallas_call(
        chip_kernel,
        out_shape=pltpu.HBM(other.shape, BF16),
        in_specs=[VMEM, VMEM],
        out_specs=HBM,
        scratch_shapes=[pltpu.VMEM(other.shape, BF16), pltpu.SemaphoreType.DMA((4,))],
        compiler_params=params(16),
        cost_estimate=cost(0, other.size * 8),
    )(mine, other)


def sum_kernel(parts_ref, out_ref):
    total = parts_ref[0].astype(F32)
    for i in range(1, parts_ref.shape[0]):
        total = total + parts_ref[i].astype(F32)
    out_ref[...] = total


def sum_parts(parts):
    return pl.pallas_call(
        sum_kernel,
        out_shape=jax.ShapeDtypeStruct(parts.shape[1:], F32),
        in_specs=[VMEM],
        out_specs=VMEM,
        compiler_params=params(16),
        cost_estimate=cost(parts.size, parts.size * 2),
    )(parts)


def update_kernel(
    share_ref, in1_ref, in2_ref, in3_ref, master_ref, first_ref, second_ref,
    spread_ref, new_master_ref, new_first_ref, new_second_ref,
):
    core, line = my_place()
    lines, _, own, width = master_ref.shape
    grad = (share_ref[...] + in1_ref[...]) + (in2_ref[...] + in3_ref[...])
    rows = lines * own
    master, first, second = adamw(
        master_ref[:, core].reshape(rows, width),
        first_ref[:, core].reshape(rows, width),
        second_ref[:, core].reshape(rows, width),
        grad,
    )
    fresh = master.astype(BF16)
    for i in range(spread_ref.shape[0]):
        spread_ref[i] = fresh
    for whole, out_ref in (
        (master, new_master_ref), (first, new_first_ref), (second, new_second_ref)
    ):
        picked = whole[:own]
        for i in range(1, lines):
            picked = jnp.where(line == i, whole[i * own : (i + 1) * own], picked)
        out_ref[...] = picked


def update(share, shares_in, master, first, second, n_dp, lines, own):
    width = master.shape[1]
    rows = [a.reshape(lines, 2, own, width) for a in (master, first, second)]
    mine = jax.ShapeDtypeStruct((own, width), F32)
    return pl.pallas_call(
        update_kernel,
        out_shape=(
            jax.ShapeDtypeStruct((n_dp, lines * own, width), BF16), mine, mine, mine,
        ),
        in_specs=[VMEM] * 7,
        out_specs=(VMEM,) * 4,
        compiler_params=params(16),
        cost_estimate=cost(20 * share.size, 60 * share.size),
    )(share, *shares_in, *rows)


def pick_kernel(other_side, index_hbm, count_hbm, table_hbm, *refs):
    if other_side:
        grad_hbm, out_ref, mine_ref, *scratch, grad_sems = refs
    else:
        out_ref, *scratch = refs
    index_ref, count_ref, table_ref, total_ref, sems = scratch
    asked = [
        pltpu.make_async_copy(index_hbm, index_ref, sems.at[0]),
        pltpu.make_async_copy(count_hbm, count_ref, sems.at[1]),
    ]
    pieces = sems.shape[0] - 2
    part = table_ref.shape[0] // pieces
    copies = [
        pltpu.make_async_copy(
            table_hbm.at[pl.ds(i * part, part)], table_ref.at[pl.ds(i * part, part)], sems.at[2 + i]
        )
        for i in range(pieces)
    ]
    for copy in asked + copies:
        copy.start()
    core, line = my_place()
    grads = load_half(grad_hbm, core, mine_ref, grad_sems) if other_side else []
    side = 1 - core if other_side else core
    askers, slots = index_ref.shape
    lines = askers // 2
    slot = lax.broadcasted_iota(I32, (1, slots), 1)
    each = lax.broadcasted_iota(I32, (1, askers), 1)
    for copy in asked:
        copy.wait()
    wanted = []
    for s in range(lines):
        asker = lax.rem(line + s, lines) * 2 + side
        used = jnp.sum(jnp.where(each == asker, count_ref[...], 0), axis=1, keepdims=True)
        wanted.append(jnp.where(slot < used, index_ref[pl.ds(asker, 1), :], -1).astype(I16))
    wanted = jnp.concatenate(wanted, axis=1)
    rows = lax.broadcasted_iota(I16, (part, lines * slots), 0)
    for i, copy in enumerate(copies):
        hit = jnp.where(rows + I16(i * part) == wanted, BF16(1), BF16(0))
        copy.wait()
        found = dot_on(hit, table_ref[i * part : (i + 1) * part, :], FIRST)
        if i > 0:
            found = found + total_ref[...]
        if i < pieces - 1:
            total_ref[...] = found
        else:
            out_ref[...] = found.astype(BF16)
    for copy in grads:
        copy.wait()


def pick(index, counts, table, grad=None):
    width = table.shape[1]
    rows = index.size // 2
    out = [jax.ShapeDtypeStruct((rows, width), BF16)]
    scratch = [
        pltpu.VMEM(index.shape, I32),
        pltpu.VMEM(counts.shape, I32),
        pltpu.VMEM(table.shape, BF16),
        pltpu.VMEM((rows, width), F32),
        pltpu.SemaphoreType.DMA((6,)),
    ]
    operands = [index, counts, table]
    if grad is not None:
        n_dp, lines, _, own, _ = grad.shape
        out.append(jax.ShapeDtypeStruct((n_dp, lines, own, width), F32))
        scratch.append(pltpu.SemaphoreType.DMA((4,)))
        operands.append(grad)
    return pl.pallas_call(
        functools.partial(pick_kernel, grad is not None),
        out_shape=tuple(out),
        in_specs=[HBM] * len(operands),
        out_specs=(VMEM,) * len(out),
        scratch_shapes=scratch,
        compiler_params=params(24),
        cost_estimate=cost(index.size * table.size, table.size * 2),
    )(*(in_hbm(a) for a in operands))


def merge_kernel(near_ref, far_ref, *out_refs):
    slots = near_ref.shape[0] // len(out_refs)
    for s, out_ref in enumerate(out_refs):
        out_ref[:slots, :] = near_ref[s * slots : (s + 1) * slots, :]
        out_ref[slots:, :] = far_ref[s * slots : (s + 1) * slots, :]


def merge(near, far, lines):
    out = jax.ShapeDtypeStruct((2 * near.shape[0] // lines, near.shape[1]), BF16)
    return pl.pallas_call(
        merge_kernel,
        out_shape=(out,) * lines,
        in_specs=[VMEM, VMEM],
        out_specs=(VMEM,) * lines,
        compiler_params=params(16),
        cost_estimate=cost(0, near.size * 8),
    )(near, far)


def cold_kernel(sample_ref, *refs):
    rows_in, rest = refs[:-8], refs[-8:]
    w_hbm, b_ref, pre_hbm, w_ref, feature_ref, held_ref, sem, out_sems = rest
    core, line = my_place()
    lines = len(rows_in)
    batch, width = feature_ref.shape
    copy = pltpu.make_async_copy(w_hbm.at[pl.ds(width, width)], w_ref, sem)
    copy.start()
    samples = []
    for s in range(lines):
        owner = lax.rem(line + lines - s, lines) * 2
        samples.append(
            jnp.concatenate(
                [sample_ref[pl.ds(owner + side, 1), :] for side in (core, 1 - core)], axis=1
            )
        )
    bag = lax.broadcasted_iota(I16, (ROWS, samples[0].shape[1]), 0)

    def pool_step(i, _):
        pool = None
        for sample, rows_ref in zip(samples, rows_in, strict=True):
            hit = bag == (sample - i * ROWS).astype(I16)
            part = dot(jnp.where(hit, BF16(1), BF16(0)), rows_ref[...])
            pool = part if pool is None else pool + part
        feature_ref[pl.ds(pl.multiple_of(i * ROWS, ROWS), ROWS), :] = pool.astype(BF16)
        return 0

    lax.fori_loop(0, batch // ROWS, pool_step, 0)
    copy.wait()

    def leave(i):
        here = pl.ds(pl.multiple_of(i * TILE, TILE), TILE)
        return pltpu.make_async_copy(held_ref.at[here], pre_hbm.at[here], out_sems.at[i])

    def step(i, _):
        here = pl.ds(pl.multiple_of(i * TILE, TILE), TILE)
        held_ref[here, :] = (dot(feature_ref[here, :], w_ref[...]) + b_ref[...]).astype(BF16)
        leave(i).start()
        return 0

    lax.fori_loop(0, batch // TILE, step, 0)
    for i in range(batch // TILE):
        leave(i).wait()


def cold_half(samples, rows_in, w_in, b_in, batch):
    hidden = w_in.shape[1]
    width = rows_in[0].shape[1]
    return pl.pallas_call(
        cold_kernel,
        out_shape=pltpu.HBM((batch, hidden), BF16),
        in_specs=[VMEM] * (len(rows_in) + 1) + [HBM, VMEM],
        out_specs=HBM,
        scratch_shapes=[
            pltpu.VMEM((width, hidden), BF16),
            pltpu.VMEM((batch, width), BF16),
            pltpu.VMEM((batch, hidden), BF16),
            pltpu.SemaphoreType.DMA(()),
            pltpu.SemaphoreType.DMA((batch // TILE,)),
        ],
        compiler_params=params(24),
        cost_estimate=cost(2 * batch * width * (hidden + samples.size), batch * hidden * 2),
    )(samples, *rows_in, in_hbm(w_in), b_in.reshape(1, hidden))


def count_kernel(low_block, own, ids_ref, lengths_ref, out_hbm, total_ref, out_ref, sems):
    core, _ = my_place()
    bags, width = out_ref.shape
    row = lax.broadcasted_iota(I32, (BAGS, BAGS), 0)
    col = lax.broadcasted_iota(I32, (BAGS, BAGS), 1)
    upto = (col <= row).astype(BF16)
    before = (col < row).astype(BF16)
    rows = lax.broadcasted_iota(I16, (width, CHUNK), 0)
    offset = F32(0.0)
    if low_block:
        offset = jnp.sum(lengths_ref[:, : low_block * BAGS].astype(F32))

    def leave(k):
        here = pl.ds(k * BAGS, BAGS)
        return pltpu.make_async_copy(out_ref.at[here], out_hbm.at[here], sems.at[k])

    for k in range(bags // BAGS):
        at = (low_block + k) * BAGS
        lengths = lengths_ref[:, at : at + BAGS].astype(F32)
        spread = jnp.broadcast_to(lengths, (LANES, BAGS)).astype(BF16)
        end = (offset + dot_on(upto, spread, LAST)).astype(I32).astype(I16)
        start = (offset + dot_on(before, spread, LAST)).astype(I32).astype(I16)
        following = offset + jnp.sum(lengths)
        lowest, highest = offset.astype(I32), following.astype(I32)
        offset = following
        total_ref[...] = jnp.zeros_like(total_ref)

        def step(j, _, start=start, end=end):
            here = pl.multiple_of(j * CHUNK, CHUNK)
            ids = ids_ref[:, pl.ds(here, CHUNK)]
            far = lax.div(ids, own) % 2 != core
            places = lax.div(ids, 2 * own) * own + lax.rem(ids, own)
            places = jnp.where(far, places + width // 2, places).astype(I16)
            hits = jnp.where(rows == places, BF16(1), BF16(0))
            lane = (here + lax.broadcasted_iota(I32, (1, CHUNK), 1)).astype(I16)
            parts = []
            for o in range(0, CHUNK, LANES):
                at_lane = lane[:, o : o + LANES]
                inside = (start <= at_lane) & (at_lane < end)
                parts.append(jnp.where(inside, BF16(1), BF16(0)))
            total_ref[...] += dot_on(jnp.concatenate(parts, axis=1), hits, LAST)
            return 0

        lax.fori_loop(lowest // CHUNK, (highest + CHUNK - 1) // CHUNK, step, 0)
        out_ref[k * BAGS : (k + 1) * BAGS, :] = total_ref[...].astype(BF16)
        leave(k).start()
    for k in range(bags // BAGS):
        leave(k).wait()


def count_matrix(ids, lengths, width, own, low_block, blocks):
    return pl.pallas_call(
        functools.partial(count_kernel, low_block, own),
        out_shape=pltpu.HBM((blocks * BAGS, width), BF16),
        in_specs=[VMEM, VMEM],
        out_specs=HBM,
        scratch_shapes=[
            pltpu.VMEM((BAGS, width), F32),
            pltpu.VMEM((blocks * BAGS, width), BF16),
            pltpu.SemaphoreType.DMA((blocks,)),
        ],
        compiler_params=params(24),
        cost_estimate=cost(3 * blocks * 2 * BAGS * CHUNK * width, 2 * blocks * BAGS * width),
    )(ids, lengths)


def own_kernel(own_ref, pre_hbm, w_in_hbm, *refs):
    counts, rest = refs[:-6], refs[-6:]
    pool_ref, count_ref, pre_ref, w_hot_ref, held_ref, sems = rest
    half = own_ref.shape[0]
    needed, later, low = [], [], 0
    for part in counts:
        here = pl.ds(low, part.shape[0])
        needed.append((part.at[:, pl.ds(0, half)], held_ref.at[here]))
        later.append((part.at[:, pl.ds(half, half)], count_ref.at[here]))
        low += part.shape[0]
    later.append((w_in_hbm.at[pl.ds(0, w_hot_ref.shape[0])], w_hot_ref))
    later.append((pre_hbm.at[pl.ds(0, pre_ref.shape[0])], pre_ref))
    copies = [
        pltpu.make_async_copy(source, target, sems.at[i])
        for i, (source, target) in enumerate(needed + later)
    ]
    for copy in copies:
        copy.start()
    for copy in copies[: len(counts)]:
        copy.wait()

    def step(i, _):
        here = pl.ds(pl.multiple_of(i * TILE, TILE), TILE)
        pool_ref[here, :] = dot(held_ref[here, :], own_ref[...])
        return 0

    lax.fori_loop(0, low // TILE, step, 0)
    for copy in copies[len(counts) :]:
        copy.wait()


def own_pool(counts, fresh_own, pre, w_in):
    half, width = fresh_own.shape
    batch, hidden = pre.shape
    return pl.pallas_call(
        own_kernel,
        out_shape=(
            pltpu.VMEM((batch, width), F32),
            pltpu.VMEM((batch, half), BF16),
            pltpu.VMEM((TILE, hidden), BF16),
            pltpu.VMEM((width, hidden), BF16),
        ),
        in_specs=[VMEM] + [HBM] * (2 + len(counts)),
        out_specs=(VMEM, VMEM, VMEM, VMEM),
        scratch_shapes=[
            pltpu.VMEM((batch, half), BF16), pltpu.SemaphoreType.DMA((2 * len(counts) + 2,))
        ],
        compiler_params=params(16),
        cost_estimate=cost(2 * batch * half * width, 3 * batch * width * 4),
    )(fresh_own, in_hbm(pre), in_hbm(w_in), *(in_hbm(c) for c in counts))


def mlp_kernel(
    pool_ref, count_ref, other_ref, w_hot_ref, first_pre_ref, pre_hbm, w_out_hbm, b_ref, out_hbm,
    hidden_ref, w_out_ref, pre_ref, out_ref, pre_sems, w_sems, out_sems,
):
    tiles = hidden_ref.shape[0] // TILE
    pieces, _, columns = w_out_ref.shape

    def load_pre(i):
        here = pl.ds(pl.multiple_of(i * TILE, TILE), TILE)
        return pltpu.make_async_copy(pre_hbm.at[here], pre_ref.at[i], pre_sems.at[i])

    def load_w(n):
        here = pl.ds(pl.multiple_of(n * columns, columns), columns)
        return pltpu.make_async_copy(w_out_hbm.at[:, here], w_out_ref.at[n], w_sems.at[n])

    def leave(n):
        here = pl.ds(pl.multiple_of(n * columns, columns), columns)
        slot = lax.rem(n, 2)
        return pltpu.make_async_copy(out_ref.at[slot], out_hbm.at[:, here], out_sems.at[slot])

    for i in range(1, tiles):
        load_pre(i).start()
    load_w(0).start()
    pre_ref[0] = first_pre_ref[...]

    def first_layer(i, _):
        here = pl.ds(pl.multiple_of(i * TILE, TILE), TILE)
        pool = pool_ref[here, :] + dot(count_ref[here, :], other_ref[...])

        @pl.when(i > 0)
        def _():
            load_pre(i).wait()

            @pl.when(i < pieces)
            def _():
                load_w(i).start()

        pre = dot(pool.astype(BF16), w_hot_ref[...]) + pre_ref[i].astype(F32)
        hidden_ref[here, :] = jnp.maximum(pre, 0.0).astype(BF16)
        return 0

    lax.fori_loop(0, tiles, first_layer, 0)

    def second_layer(n, _):
        load_w(n).wait()

        @pl.when(n >= 2)
        def _():
            leave(n - 2).wait()

        here = pl.ds(pl.multiple_of(n * columns, columns), columns)
        out_ref[lax.rem(n, 2)] = dot(hidden_ref[...], w_out_ref[n]) + b_ref[:, here]
        leave(n).start()
        return 0

    lax.fori_loop(0, pieces, second_layer, 0)
    leave(pieces - 2).wait()
    leave(pieces - 1).wait()


def mlp(pool, counts, fresh_other, w_hot, first_pre, pre, w_out, b_out):
    batch, hidden = pre.shape
    wide = w_out.shape[1]
    half, width = fresh_other.shape
    pieces = wide // PIECE
    return pl.pallas_call(
        mlp_kernel,
        out_shape=jax.ShapeDtypeStruct((batch, wide), F32),
        in_specs=[VMEM] * 5 + [HBM, HBM, VMEM],
        out_specs=HBM,
        scratch_shapes=[
            pltpu.VMEM((batch, hidden), BF16),
            pltpu.VMEM((pieces, hidden, PIECE), BF16),
            pltpu.VMEM((batch // TILE, TILE, hidden), BF16),
            pltpu.VMEM((2, batch, PIECE), F32),
            pltpu.SemaphoreType.DMA((batch // TILE,)),
            pltpu.SemaphoreType.DMA((pieces,)),
            pltpu.SemaphoreType.DMA((2,)),
        ],
        compiler_params=params(36),
        cost_estimate=cost(
            2 * batch * (half * width + width * hidden + hidden * wide), batch * wide * 4
        ),
    )(
        pool, counts, fresh_other, w_hot, first_pre, in_hbm(pre), in_hbm(w_out),
        b_out.reshape(1, wide),
    )


def on_device(
    hot_grad,
    first_moment,
    second_moment,
    hot_master,
    hot_ids,
    hot_lengths,
    cold_table,
    cold_index,
    cold_count,
    cold_sample,
    w_in,
    b_in,
    w_out,
    b_out,
):
    width = cold_table.shape[1]
    batch = hot_lengths.shape[2]
    hot = hot_grad.shape[2]
    n_dp, n_table = lax.axis_size("dp"), lax.axis_size("table")
    lines = n_table // 2
    own = hot // (n_dp * n_table)
    swap = [(i, i ^ 1) for i in range(n_table)]

    def along(array, step):
        pairs = [(i, (i + 2 * step) % n_table) for i in range(n_table)]
        return lax.ppermute(array, "table", pairs)

    grad = hot_grad[0, 0].reshape(n_dp, lines, 2, own, width)
    send = other_half(grad)
    other = lax.ppermute(send, "table", swap)
    index, counts = cold_index[0, 0], cold_count[0]
    (index_far,) = after(send, index)
    far, mine = pick(index_far, counts, cold_table, grad)
    chip = chip_rows(mine, other)

    parts = lax.all_to_all(
        chip.reshape(n_dp, lines * own, width), "dp", split_axis=0, concat_axis=0, tiled=True
    )
    index_near, far = after(chip, index, far)
    far_in = lax.ppermute(far, "table", swap)
    (near,) = pick(index_near, counts, cold_table)
    blocks = merge(near, far_in, lines)
    rows_in = [along(blocks[s], s) if s in (1, lines - 1) else blocks[s] for s in range(lines)]

    ids, lengths = hot_ids[0], hot_lengths[0]
    blocks_in_all = batch // BAGS
    early = blocks_in_all // 2
    (ids_now,) = after(blocks[0], ids)
    count_low = count_matrix(ids_now, lengths, hot, own, 0, early)
    (parts,) = after(count_low, parts)
    share = sum_parts(parts)
    shares_in = [along(share, s) for s in (1, 3, 2)]
    spread, new_master, new_first, new_second = update(
        share, shares_in, hot_master, first_moment, second_moment, n_dp, lines, own
    )
    fresh_own = lax.all_to_all(spread, "dp", split_axis=0, concat_axis=0, tiled=True)
    samples, ids_late, *further = after(spread, cold_sample[0, 0], ids, *rows_in[2:-1])
    rows_in[2:-1] = [along(block, 2 + s) for s, block in enumerate(further)]
    count_high = count_matrix(ids_late, lengths, hot, own, early, blocks_in_all - early)
    pre = cold_half(samples, rows_in, w_in, b_in, batch)
    fresh_own, *_ = lax.optimization_barrier((fresh_own, pre, count_high))
    fresh_own = fresh_own.reshape(hot // 2, width)
    fresh_other = lax.ppermute(fresh_own, "table", swap)
    pool, counts_other, first_pre, w_hot = own_pool(
        [count_low, count_high], fresh_own, pre, w_in
    )
    fresh_other, pool = lax.optimization_barrier((fresh_other, pool))
    result = mlp(pool, counts_other, fresh_other, w_hot, first_pre, pre, w_out, b_out)
    return (result[None, None], new_master, new_first, new_second)


def solution(mesh):
    return jax.shard_map(
        on_device,
        mesh=mesh,
        in_specs=(
            P("dp", "table", None, None),
            P("dp", None),
            P("dp", None),
            P("dp", None),
            P("dp", "table", None),
            P("dp", "table", None),
            P("table", None),
            P("dp", "table", None, None),
            P("dp", "table", None),
            P("dp", "table", None, None),
            P(),
            P(),
            P(),
            P(),
        ),
        out_specs=(
            P("dp", "table", None, None),
            P(("dp", "table"), None),
            P(("dp", "table"), None),
            P(("dp", "table"), None),
        ),
        check_vma=False,
    )
```
